512 devices in a mesh: dp: 32 (over x_lo, z), tensor: 16 (over y, x_hi, core).
Axes of the slice: x: 4 (x_hi: 2, x_lo: 2; x = x_hi * 2 + x_lo), y: 4, z: 16, core: 2. Of those that a mesh axis runs over, the one named last changes fastest.
Arguments:
- learn_acts: bfloat16 [16384, 8192], P('dp', 'tensor'), may hold values from -6 to 6
- cotangent: bfloat16 [16384, 1024], P('dp'), may hold values from -6 to 6
- base_weight: bfloat16 [8192, 1024], P('tensor'), may hold values from -0.0625 to 0.0625
- down_factor: float32 [64, 8192], P(None, 'tensor'), may hold values from -0.0625 to 0.0625
- up_factor: float32 [1024, 64], replicated, may hold values from -0.75 to 0.75
- decode_acts: bfloat16 [16384, 8192], P('dp', 'tensor'), may hold values from -6 to 6
Outputs:
- grad_acts: bfloat16 [16384, 8192], P('dp', 'tensor')
- new_down: float32 [64, 8192], P('dp', 'tensor')
- new_up: float32 [1024, 64], P(('dp', 'tensor'))
- decoded: bfloat16 [16384, 1024], P('dp')
The draws below stay inside these ranges and needn't reach their ends.
All inputs are finite; a program needn't handle non-finite values.
Results may differ from the reference program's by a relative error of at most 0.025.
Values may be sent and summed in bfloat16 or wider, within the bound.
A program may use at most 64 MiB of HBM per device.

```python
import jax
import jax.numpy as jnp
from jax import lax

D = 8192
KV = 1024
R = 64
TOKENS = 16384
DEC_ROWS = 16384
N_TENSOR = 16


def with_spikes(entries, rng, source, target, shards_of, factor):
    owner, partner = [(jnp.arange(entries.shape[position]) // (entries.shape[position] // shards_of)).reshape([-1 if axis == position else 1 for axis in range(entries.ndim)]) for position in (source, target)]
    chosen = jax.random.permutation(rng, shards_of)[partner]
    strong = (owner == chosen) | (owner == (partner + shards_of // 2) % shards_of)
    return jnp.where(strong, factor * entries, entries)


def steps_of(rng, extent, cuts, low, top_value):
    gain = 1.0
    for dim, shards_of in cuts:
        heights = jax.random.uniform(jax.random.fold_in(jax.random.fold_in(rng, 6), dim), (shards_of,), jnp.float32, low / len(cuts), top_value / len(cuts))
        gain = gain * jnp.repeat(jnp.exp(heights), extent[dim] // shards_of).reshape((-1,) + (1,) * (len(extent) - 1 - dim))
    return gain


def normal_values(stream_key, shape, spread, limit, cuts=(), dtype=jnp.bfloat16):
    result = spread * jax.random.normal(stream_key, shape, jnp.float32)
    if cuts:
        result = result * steps_of(stream_key, shape, cuts, -0.22, 0.18)
    return jnp.clip(result, -limit, limit).astype(dtype)


def heavy_noise(own_key, shape, scale, limit, cuts, heavy, dtype=jnp.bfloat16):
    array = scale * jax.random.normal(own_key, shape, jnp.float32)
    if cuts:
        array = array * steps_of(own_key, shape, cuts, -0.22, 0.18)
    return jnp.clip(with_spikes(array, jax.random.fold_in(own_key, 3), *heavy), -limit, limit).astype(dtype)


def setup_inputs(seed: int = 0) -> dict:
    seeds = jax.random.split(jax.random.key(seed), 7)
    return {
        "learn_acts": normal_values(seeds[0], (TOKENS, D), 1.0, 6.0, ((0, 32), (1, 16))),
        "cotangent": heavy_noise(seeds[1], (TOKENS, KV), 1.0, 6.0, ((0, 32),), (0, 1, 32, 2.75)),
        "base_weight": normal_values(seeds[2], (D, KV), D ** -0.5, 0.0625, ((0, 16),)),
        "down_factor": normal_values(seeds[3], (R, D), D ** -0.5, 0.0625, ((1, 16),), jnp.float32),
        "up_factor": normal_values(seeds[4], (KV, R), R ** -0.5, 0.75, (), jnp.float32),
        "decode_acts": normal_values(seeds[5], (DEC_ROWS, D), 1.0, 6.0, ((0, 32), (1, 16))),
    }


rate_down = 0.2
rate_up = 3.0


def blockwise(left, right):
    width = left.shape[1] // N_TENSOR
    total = jnp.zeros((left.shape[0], right.shape[1]), jnp.float32)
    for block_id in range(N_TENSOR):
        piece = left[:, block_id * width:(block_id + 1) * width]
        rows = right[block_id * width:(block_id + 1) * width, :]
        partial_sum = jnp.dot(piece, rows, preferred_element_type=jnp.float32).astype(jnp.bfloat16)
        total = total + partial_sum.astype(jnp.float32)
    return total.astype(jnp.bfloat16)


def reference(learn_acts, cotangent, base_weight, down_factor, up_factor, decode_acts):
    down16 = down_factor.astype(jnp.bfloat16)
    up16 = up_factor.astype(jnp.bfloat16)
    low_in = blockwise(learn_acts, down16.T)
    low_out = jnp.dot(cotangent, up16, preferred_element_type=jnp.float32).astype(jnp.bfloat16)
    grad_acts = (jnp.dot(cotangent, base_weight.T, preferred_element_type=jnp.float32)
                 + jnp.dot(low_out, down16, preferred_element_type=jnp.float32)).astype(jnp.bfloat16)
    grad_down = jnp.dot(low_out.T, learn_acts, preferred_element_type=jnp.float32) / TOKENS
    grad_up = jnp.dot(cotangent.T, low_in, preferred_element_type=jnp.float32) / TOKENS
    new_down = down_factor - rate_down * grad_down
    new_up = up_factor - rate_up * grad_up
    merged = (base_weight.astype(jnp.float32)
              + jnp.dot(new_down.T, new_up.T, precision=lax.Precision.HIGHEST)).astype(jnp.bfloat16)
    decoded = blockwise(decode_acts, merged)
    return grad_acts, new_down, new_up, decoded
```

```python
import jax
import jax.numpy as jnp
from jax import lax
from jax.experimental import pallas as pl
from jax.experimental.pallas import tpu as pltpu
from jax.sharding import PartitionSpec as P

rate_down = 0.2
rate_up = 3.0

NZ = 16
GZ = 4
NA = 8
NB = 4
NC = 8

BF = jnp.bfloat16
F32 = jnp.float32

(D_A, D_B, D_C, U_PAIR, U_RS, U_A, U_B, U_AG, U_PAIR2,
 M_PAIR, M_RS, M_AG, M_PAIR2, L_PAIR, L_ALL, L_PAIR2) = range(16)
(I_COT, I_UP, I_LEARN, I_DOWN, I_DEC, I_BASE,
 O_GA, O_ND, O_NU, O_NUT, O_LD, O_M) = range(12)


def dot(a, b, ca, cb):
    return lax.dot_general(a, b, (((ca,), (cb,)), ((), ())), preferred_element_type=F32)


def comm_kernel(
    learn_h, cot_h, base_h, down_h, up_h, dec_h,
    ga_h, nd_h, nu_h, nut_h, ld_h, m_h,
    learn, cot, base, down, up, dec, ga,
    lowout, td_send, d_a, d_b, d_c, ndown, nd_out,
    g32, u_send, u_prec, u_sum, u_rs, u_a, u_b, u_fin, upt, nupt16, nup, nu_out,
    m_send, m_keep, m_prec, m_sum, m_rs, m_fin,
    l32, l_send, l_prec, l_all, l_fin,
    ssem, rsem, lsem,
):
    d = lax.axis_index("dp")
    t = lax.axis_index("tensor")
    x = d // NZ
    z = d % NZ
    zb = z // GZ
    za = z % GZ
    a = x * GZ + za
    q = t // 2
    c = t % 2
    oc = 1 - c
    total = 16384.0

    def load(src, dst, i):
        cp = pltpu.make_async_copy(src, dst, lsem.at[i])
        cp.start()
        return cp

    cp_cot = load(cot_h, cot, I_COT)
    cp_up = load(up_h, up, I_UP)
    cp_learn = load(learn_h, learn, I_LEARN)
    cp_down = load(down_h, down, I_DOWN)
    cp_dec = load(dec_h, dec, I_DEC)
    cp_base = load(base_h, base, I_BASE)

    def near(k):
        other = (a + k) % NA
        return other, {"dp": (other // GZ) * NZ + zb * GZ + other % GZ, "tensor": t}

    def far(k):
        return {"dp": x * NZ + ((zb + k) % NB) * GZ + za, "tensor": t}

    def chip(k):
        other = (q + k) % NC
        return other, {"dp": d, "tensor": other * 2 + c}

    pair = {"dp": d, "tensor": q * 2 + oc}

    barrier = pltpu.get_barrier_semaphore()

    def greet(dev):
        pl.semaphore_signal(barrier, inc=1, device_id=dev, device_id_type=pl.DeviceIdType.MESH)

    def hello_near(k, _):
        greet(near(k)[1])
        return 0

    def hello_far(k, _):
        greet(far(k))
        return 0

    def hello_chip(k, _):
        greet(chip(k)[1])
        return 0

    lax.fori_loop(1, NB, hello_far, 0)
    lax.fori_loop(1, NA, hello_near, 0)
    lax.fori_loop(1, NC, hello_chip, 0)
    greet(pair)

    def remote(src, dst, i, dev):
        return pltpu.make_async_remote_copy(
            src_ref=src, dst_ref=dst, send_sem=ssem.at[i], recv_sem=rsem.at[i],
            device_id=dev, device_id_type=pl.DeviceIdType.MESH,
        )

    def arrived(ref, i):
        remote(ref, ref, i, pair).wait_recv()

    def sent(ref, i):
        remote(ref, ref, i, pair).wait_send()

    def to_near(i, src, dst):
        def step(k, _):
            other, dev = near(k)
            remote(src(other), dst, i, dev).start()
            return 0
        lax.fori_loop(1, NA, step, 0)

    def to_far(i, src, dst):
        def step(k, _):
            remote(src, dst, i, far(k)).start()
            return 0
        lax.fori_loop(1, NB, step, 0)

    def to_chips(i, src, dst):
        def step(k, _):
            other, dev = chip(k)
            remote(src(other), dst, i, dev).start()
            return 0
        lax.fori_loop(1, NC, step, 0)

    def total_of(ref):
        acc = ref[0].astype(F32)
        for k in range(1, ref.shape[0]):
            acc = acc + ref[k].astype(F32)
        return acc

    def two_rows(ref, block, first):
        rows = ref[pl.ds(pl.multiple_of(block * 8, 8), 8), :]
        at = lax.broadcasted_iota(jnp.int32, rows.shape, 0)
        picked = [
            jnp.sum(jnp.where(at == first + k, rows, 0.0), axis=0, keepdims=True) for k in range(2)
        ]
        return jnp.concatenate(picked, axis=0)

    cp_cot.wait()
    cp_up.wait()
    lowout[...] = dot(cot[...], up[...].astype(BF), 1, 0).astype(BF)
    cp_learn.wait()
    term = dot(lowout[...], learn[...], 0, 0).astype(BF)
    for k in range(NA):
        i, j = k // 4, k % 4
        td_send[k] = term[32 * i:32 * i + 32, 128 * j:128 * j + 128]
    d_a[a] = td_send[a]

    pl.semaphore_wait(barrier, (NB - 1) + (NA - 1) + (NC - 1) + 1)
    to_near(D_A, lambda o: td_send.at[o], d_a.at[a])

    cp_down.wait()
    down16 = down[...].astype(BF)
    low_in = dot(down16, learn[...], 1, 1).astype(BF)
    term_up = dot(low_in, cot[...], 1, 0)
    for i in range(2):
        for j in range(NC):
            g32[i, j] = term_up[32 * i:32 * i + 32, 128 * j:128 * j + 128]
    u_send[...] = g32[oc].astype(BF)
    remote(u_send, u_prec, U_PAIR, pair).start()

    cp_dec.wait()
    cp_base.wait()

    def other_half(r, _):
        rows = pl.ds(pl.multiple_of(r * 128, 128), 128)
        cols = pl.ds(pl.multiple_of(oc * 512, 512), 512)
        m_send[rows, :] = dot(dec[rows, :], base[:, cols], 1, 0).astype(BF)
        return 0

    def own_half(r, _):
        rows = pl.ds(pl.multiple_of(r * 128, 128), 128)
        cols = pl.ds(pl.multiple_of(c * 512, 512), 512)
        m_keep[rows, :] = dot(dec[rows, :], base[:, cols], 1, 0)
        return 0

    lax.fori_loop(0, 4, other_half, 0)
    remote(m_send, m_prec, M_PAIR, pair).start()

    arrived(u_prec, U_PAIR)
    u_sum[...] = (g32[c] + u_prec[...].astype(F32)).astype(BF)
    u_rs[q] = u_sum[q]
    to_chips(U_RS, lambda o: u_sum.at[o], u_rs.at[q])

    lax.fori_loop(0, 4, own_half, 0)
    arrived(m_prec, M_PAIR)

    def add_half(r, _):
        rows = pl.ds(pl.multiple_of(r * 64, 64), 64)
        m_sum[r] = (m_keep[rows, :] + m_prec[rows, :].astype(F32)).astype(BF)
        return 0

    lax.fori_loop(0, NC, add_half, 0)
    m_rs[q] = m_sum[q]

    arrived(d_a.at[pl.ds(0, NA - 1)], D_A)
    d_b[zb] = total_of(d_a).astype(BF)
    to_far(D_B, d_b.at[zb], d_b.at[zb])

    to_chips(M_RS, lambda o: m_sum.at[o], m_rs.at[q])

    def acts(r, _):
        rows = pl.ds(pl.multiple_of(r * 128, 128), 128)
        ga[rows, :] = (
            dot(cot[rows, :], base[...], 1, 1) + dot(lowout[rows, :], down[...].astype(BF), 1, 0)
        ).astype(BF)
        return 0

    lax.fori_loop(0, 4, acts, 0)
    cp_ga = load(ga, ga_h, O_GA)
    upt[...] = up[...].T

    arrived(u_rs.at[pl.ds(0, NC - 1)], U_RS)
    u_a[a] = total_of(u_rs).astype(BF)
    to_near(U_A, lambda o: u_a.at[a], u_a.at[a])

    arrived(u_a.at[pl.ds(0, NA - 1)], U_A)
    u_b[zb] = total_of(u_a).astype(BF)
    to_far(U_B, u_b.at[zb], u_b.at[zb])

    arrived(d_b.at[pl.ds(0, NB - 1)], D_B)
    d_c[a] = total_of(d_b).astype(BF)
    to_near(D_C, lambda o: d_c.at[a], d_c.at[a])

    my_rows = pl.ds(pl.multiple_of(q * 64, 64), 64)
    arrived(m_rs.at[pl.ds(0, NC - 1)], M_RS)
    m_fin[c, my_rows, :] = total_of(m_rs).astype(BF)
    to_chips(M_AG, lambda o: m_fin.at[c, my_rows], m_fin.at[c, my_rows])

    arrived(d_c.at[pl.ds(0, NA - 1)], D_C)
    for k in range(NA):
        i, j = k // 4, k % 4
        rows, cols = pl.ds(32 * i, 32), pl.ds(128 * j, 128)
        grad = d_c[k].astype(F32) / total
        ndown[rows, cols] = down[rows, cols] - rate_down * grad
    l32[...] = dot(ndown[...].astype(BF), dec[...], 1, 1)
    l_send[...] = l32[pl.ds(pl.multiple_of(oc * 32, 32), 32), :].astype(BF)
    remote(l_send, l_prec, L_PAIR, pair).start()
    nd_out[...] = two_rows(ndown, d // 4, 2 * (d % 4))
    cp_nd = load(nd_out, nd_h, O_ND)
    arrived(l_prec, L_PAIR)
    l_all[q] = (l32[pl.ds(pl.multiple_of(c * 32, 32), 32), :] + l_prec[...].astype(F32)).astype(BF)
    to_chips(L_ALL, lambda o: l_all.at[q], l_all.at[q])

    arrived(u_b.at[pl.ds(0, NB - 1)], U_B)
    u_fin[c, q] = total_of(u_b).astype(BF)
    to_chips(U_AG, lambda o: u_fin.at[c, q], u_fin.at[c, q])

    arrived(m_fin.at[c, pl.ds(0, 448)], M_AG)
    remote(m_fin.at[c], m_fin.at[c], M_PAIR2, pair).start()

    arrived(u_fin.at[c, pl.ds(0, NC - 1)], U_AG)
    remote(u_fin.at[c], u_fin.at[c], U_PAIR2, pair).start()

    arrived(m_fin.at[oc], M_PAIR2)
    cp_m = load(m_fin, m_h, O_M)

    arrived(u_fin.at[oc], U_PAIR2)
    for i in range(2):
        for j in range(NC):
            rows, cols = pl.ds(32 * i, 32), pl.ds(128 * j, 128)
            grad = u_fin[i, j].astype(F32) / total
            upt[rows, cols] = upt[rows, cols] - rate_up * grad
    nupt16[...] = upt[...].astype(BF)
    cp_nut = load(nupt16, nut_h, O_NUT)
    nup[...] = upt[...].T
    nu_out[...] = two_rows(nup, d * 4 + t // 4, 2 * (t % 4))
    cp_nu = load(nu_out, nu_h, O_NU)

    half = pl.ds(pl.multiple_of(c * 32, 32), 32)
    arrived(l_all.at[pl.ds(0, NC - 1)], L_ALL)
    l_fin[half, :] = total_of(l_all).astype(BF)
    remote(l_fin.at[half], l_fin.at[half], L_PAIR2, pair).start()
    arrived(l_fin.at[half], L_PAIR2)
    cp_ld = load(l_fin, ld_h, O_LD)

    m_part = m_fin.at[c, pl.ds(0, 448)]
    for ref, i in (
        (td_send.at[pl.ds(0, NA - 1)], D_A), (d_b.at[pl.ds(0, NB - 1)], D_B),
        (d_c.at[pl.ds(0, NA - 1)], D_C), (u_send, U_PAIR), (u_rs.at[pl.ds(0, NC - 1)], U_RS),
        (u_a.at[pl.ds(0, NA - 1)], U_A), (u_b.at[pl.ds(0, NB - 1)], U_B),
        (u_fin.at[c, pl.ds(0, NC - 1)], U_AG), (u_fin.at[c], U_PAIR2), (m_send, M_PAIR),
        (m_rs.at[pl.ds(0, NC - 1)], M_RS), (m_part, M_AG), (m_fin.at[c], M_PAIR2),
        (l_send, L_PAIR), (l_all.at[pl.ds(0, NC - 1)], L_ALL), (l_fin.at[half], L_PAIR2),
    ):
        sent(ref, i)
    for cp in (cp_ga, cp_nd, cp_m, cp_nut, cp_nu, cp_ld):
        cp.wait()


def finish_kernel(m_ref, ld_ref, nut_ref, ga_in, nd_in, nu_in, dec_out, ga_out, nd_out, nu_out, sem):
    step = pl.program_id(0)

    def copies():
        return [
            pltpu.make_async_copy(s, o, sem.at[i])
            for i, (s, o) in enumerate(((ga_in, ga_out), (nd_in, nd_out), (nu_in, nu_out)))
        ]

    @pl.when(step == 0)
    def _():
        for cp in copies():
            cp.start()

    corr = dot(ld_ref[...], nut_ref[...], 0, 0)
    for h in range(2):
        cols = slice(512 * h, 512 * h + 512)
        dec_out[:, cols] = (m_ref[h].astype(F32) + corr[:, cols]).astype(BF)

    @pl.when(step == pl.num_programs(0) - 1)
    def _():
        for cp in copies():
            cp.wait()


def body(learn_acts, cotangent, base_weight, down_factor, up_factor, decode_acts):
    any_ = pl.BlockSpec(memory_space=pl.ANY)
    V = pltpu.VMEM
    sds = jax.ShapeDtypeStruct
    ga, nd, nu, nut, ld, m = pl.pallas_call(
        comm_kernel,
        out_shape=(
            sds((512, 512), BF), sds((2, 512), F32), sds((2, 64), F32),
            sds((64, 1024), BF), sds((64, 512), BF), sds((2, 512, 512), BF),
        ),
        in_specs=[any_] * 6,
        out_specs=(any_,) * 6,
        scratch_shapes=[
            V((512, 512), BF), V((512, 1024), BF), V((512, 1024), BF), V((64, 512), F32),
            V((1024, 64), F32), V((512, 512), BF), V((512, 512), BF),
            V((512, 64), BF), V((NA, 32, 128), BF), V((NA, 32, 128), BF), V((NB, 32, 128), BF),
            V((NA, 32, 128), BF), V((64, 512), F32), V((2, 512), F32),
            V((2, NC, 32, 128), F32), V((NC, 32, 128), BF), V((NC, 32, 128), BF),
            V((NC, 32, 128), BF), V((NC, 32, 128), BF), V((NA, 32, 128), BF), V((NB, 32, 128), BF),
            V((2, NC, 32, 128), BF), V((64, 1024), F32), V((64, 1024), BF), V((1024, 64), F32),
            V((2, 64), F32),
            V((512, 512), BF), V((512, 512), F32), V((512, 512), BF), V((NC, 64, 512), BF),
            V((NC, 64, 512), BF), V((2, 512, 512), BF),
            V((64, 512), F32), V((32, 512), BF), V((32, 512), BF), V((NC, 32, 512), BF),
            V((64, 512), BF),
            pltpu.SemaphoreType.DMA((16,)), pltpu.SemaphoreType.DMA((16,)),
            pltpu.SemaphoreType.DMA((12,)),
        ],
        compiler_params=pltpu.CompilerParams(
            collective_id=0, has_side_effects=True, vmem_limit_bytes=48 * 1024 * 1024
        ),
        name="adapter_step",
    )(learn_acts, cotangent, base_weight, down_factor, up_factor, decode_acts)
    tile = 128
    decoded, ga, nd, nu = pl.pallas_call(
        finish_kernel,
        grid=(512 // tile,),
        out_shape=(
            sds((512, 1024), BF), sds((512, 512), BF), sds((2, 512), F32), sds((2, 64), F32),
        ),
        in_specs=[
            pl.BlockSpec((2, tile, 512), lambda i: (0, i, 0)),
            pl.BlockSpec((64, tile), lambda i: (0, i)),
            pl.BlockSpec((64, 1024), lambda i: (0, 0)),
            any_, any_, any_,
        ],
        out_specs=(pl.BlockSpec((tile, 1024), lambda i: (i, 0)), any_, any_, any_),
        scratch_shapes=[pltpu.SemaphoreType.DMA((3,))],
        name="finish",
    )(m, ld, nut, ga, nd, nu)
    return (ga, nd, nu, decoded)


def solution(mesh):
    in_specs = (
        P("dp", "tensor"),
        P("dp", None),
        P("tensor", None),
        P(None, "tensor"),
        P(),
        P("dp", "tensor"),
    )
    out_specs = (P("dp", "tensor"), P("dp", "tensor"), P(("dp", "tensor"), None), P("dp", None))
    return jax.shard_map(body, mesh=mesh, in_specs=in_specs, out_specs=out_specs, check_vma=False)
```

```python
import jax
import jax.numpy as jnp
from jax import lax
from jax.experimental import pallas as pl
from jax.experimental.pallas import tpu as pltpu
from jax.sharding import PartitionSpec as P

rate_down = 0.2
rate_up = 3.0

NZ = 16
GZ = 4
NA = 8
NB = 4
NC = 8

BF = jnp.bfloat16
F32 = jnp.float32

(D_A, D_B, D_C, U_PAIR, U_RS, U_A, U_B, U_AG, U_PAIR2,
 M_PAIR, M_RS, M_AG, M_PAIR2, L_PAIR, L_ALL, L_PAIR2) = range(16)
(I_COT, I_UP, I_LEARN, I_DOWN, I_DEC, I_BASE,
 O_GA, O_ND, O_NU, O_NUT, O_LD, O_M) = range(12)


def dot(a, b, ca, cb):
    return lax.dot_general(a, b, (((ca,), (cb,)), ((), ())), preferred_element_type=F32)


def comm_kernel(
    learn_h, cot_h, base_h, down_h, up_h, dec_h,
    ga_h, nd_h, nu_h, nut_h, ld_h, m_h,
    learn, cot, base, down, dec, ga,
    lowout, td_send, d_a, d_b, d_c, ndown, nd_out,
    g32, u_send, u_prec, u_sum, u_rs, u_a, u_b, u_fin, upt, nupt16, nup, nu_out,
    m_send, m_keep, m_prec, m_sum, m_rs, m_fin,
    l32, l_send, l_prec, l_all, l_fin,
    ssem, rsem, lsem,
):
    d = lax.axis_index("dp")
    t = lax.axis_index("tensor")
    x = d // NZ
    z = d % NZ
    zb = z // GZ
    za = z % GZ
    a = x * GZ + za
    q = t // 2
    c = t % 2
    oc = 1 - c
    total = 16384.0

    def load(src, dst, i):
        cp = pltpu.make_async_copy(src, dst, lsem.at[i])
        cp.start()
        return cp

    cp_cot = load(cot_h, cot, I_COT)
    cp_up = load(up_h, upt, I_UP)
    cp_learn = load(learn_h, learn, I_LEARN)
    cp_down = load(down_h, down, I_DOWN)
    cp_dec = load(dec_h, dec, I_DEC)
    cp_base = load(base_h, base, I_BASE)

    def near(k):
        other = (a + k) % NA
        return other, {"dp": (other // GZ) * NZ + zb * GZ + other % GZ, "tensor": t}

    def far(k):
        return {"dp": x * NZ + ((zb + k) % NB) * GZ + za, "tensor": t}

    def chip(k):
        other = (q + k) % NC
        return other, {"dp": d, "tensor": other * 2 + c}

    pair = {"dp": d, "tensor": q * 2 + oc}

    barrier = pltpu.get_barrier_semaphore()

    def greet(dev):
        pl.semaphore_signal(barrier, inc=1, device_id=dev, device_id_type=pl.DeviceIdType.MESH)

    def hello_near(k, _):
        greet(near(k)[1])
        return 0

    def hello_far(k, _):
        greet(far(k))
        return 0

    def hello_chip(k, _):
        greet(chip(k)[1])
        return 0

    lax.fori_loop(1, NB, hello_far, 0)
    lax.fori_loop(1, NA, hello_near, 0)
    lax.fori_loop(1, NC, hello_chip, 0)
    greet(pair)

    def remote(src, dst, i, dev):
        return pltpu.make_async_remote_copy(
            src_ref=src, dst_ref=dst, send_sem=ssem.at[i], recv_sem=rsem.at[i],
            device_id=dev, device_id_type=pl.DeviceIdType.MESH,
        )

    def arrived(ref, i):
        remote(ref, ref, i, pair).wait_recv()

    def sent(ref, i):
        remote(ref, ref, i, pair).wait_send()

    def to_near(i, src, dst):
        def step(k, _):
            other, dev = near(k)
            remote(src(other), dst, i, dev).start()
            return 0
        lax.fori_loop(1, NA, step, 0)

    def to_far(i, src, dst):
        def step(k, _):
            remote(src, dst, i, far(k)).start()
            return 0
        lax.fori_loop(1, NB, step, 0)

    def to_chips(i, src, dst):
        def step(k, _):
            other, dev = chip(k)
            remote(src(other), dst, i, dev).start()
            return 0
        lax.fori_loop(1, NC, step, 0)

    def total_of(ref):
        acc = ref[0].astype(F32)
        for k in range(1, ref.shape[0]):
            acc = acc + ref[k].astype(F32)
        return acc

    def two_rows(ref, block, first):
        rows = ref[pl.ds(pl.multiple_of(block * 8, 8), 8), :]
        at = lax.broadcasted_iota(jnp.int32, rows.shape, 0)
        picked = [
            jnp.sum(jnp.where(at == first + k, rows, 0.0), axis=0, keepdims=True) for k in range(2)
        ]
        return jnp.concatenate(picked, axis=0)

    cp_cot.wait()
    cp_up.wait()
    lowout[...] = dot(cot[...], upt[...].astype(BF), 1, 1).astype(BF)
    cp_learn.wait()
    term = dot(lowout[...], learn[...], 0, 0).astype(BF)
    for k in range(NA):
        i, j = k // 4, k % 4
        td_send[k] = term[32 * i:32 * i + 32, 128 * j:128 * j + 128]
    d_a[a] = td_send[a]

    pl.semaphore_wait(barrier, (NB - 1) + (NA - 1) + (NC - 1) + 1)
    to_near(D_A, lambda o: td_send.at[o], d_a.at[a])

    cp_down.wait()
    down16 = down[...].astype(BF)
    low_in = dot(down16, learn[...], 1, 1).astype(BF)
    term_up = dot(low_in, cot[...], 1, 0)
    for i in range(2):
        for j in range(NC):
            g32[i, j] = term_up[32 * i:32 * i + 32, 128 * j:128 * j + 128]
    u_send[...] = g32[oc].astype(BF)
    remote(u_send, u_prec, U_PAIR, pair).start()

    cp_dec.wait()
    cp_base.wait()

    def other_half(r, _):
        rows = pl.ds(pl.multiple_of(r * 128, 128), 128)
        cols = pl.ds(pl.multiple_of(oc * 512, 512), 512)
        m_send[rows, :] = dot(dec[rows, :], base[:, cols], 1, 0).astype(BF)
        return 0

    def own_half(r, _):
        rows = pl.ds(pl.multiple_of(r * 128, 128), 128)
        cols = pl.ds(pl.multiple_of(c * 512, 512), 512)
        m_keep[rows, :] = dot(dec[rows, :], base[:, cols], 1, 0)
        return 0

    lax.fori_loop(0, 4, other_half, 0)
    remote(m_send, m_prec, M_PAIR, pair).start()

    arrived(u_prec, U_PAIR)
    u_sum[...] = (g32[c] + u_prec[...].astype(F32)).astype(BF)
    u_rs[q] = u_sum[q]
    to_chips(U_RS, lambda o: u_sum.at[o], u_rs.at[q])

    lax.fori_loop(0, 4, own_half, 0)
    arrived(m_prec, M_PAIR)

    def add_half(r, _):
        rows = pl.ds(pl.multiple_of(r * 64, 64), 64)
        m_sum[r] = (m_keep[rows, :] + m_prec[rows, :].astype(F32)).astype(BF)
        return 0

    lax.fori_loop(0, NC, add_half, 0)
    m_rs[q] = m_sum[q]

    arrived(d_a.at[pl.ds(0, NA - 1)], D_A)
    d_b[zb] = total_of(d_a).astype(BF)
    to_far(D_B, d_b.at[zb], d_b.at[zb])

    to_chips(M_RS, lambda o: m_sum.at[o], m_rs.at[q])

    def acts(r, _):
        rows = pl.ds(pl.multiple_of(r * 128, 128), 128)
        ga[rows, :] = (
            dot(cot[rows, :], base[...], 1, 1) + dot(lowout[rows, :], down[...].astype(BF), 1, 0)
        ).astype(BF)
        return 0

    lax.fori_loop(0, 4, acts, 0)
    cp_ga = load(ga, ga_h, O_GA)

    arrived(u_rs.at[pl.ds(0, NC - 1)], U_RS)
    u_a[a] = total_of(u_rs).astype(BF)
    to_near(U_A, lambda o: u_a.at[a], u_a.at[a])

    arrived(u_a.at[pl.ds(0, NA - 1)], U_A)
    u_b[zb] = total_of(u_a).astype(BF)
    to_far(U_B, u_b.at[zb], u_b.at[zb])

    arrived(d_b.at[pl.ds(0, NB - 1)], D_B)
    d_c[a] = total_of(d_b).astype(BF)
    to_near(D_C, lambda o: d_c.at[a], d_c.at[a])

    my_rows = pl.ds(pl.multiple_of(q * 64, 64), 64)
    arrived(m_rs.at[pl.ds(0, NC - 1)], M_RS)
    m_fin[c, my_rows, :] = total_of(m_rs).astype(BF)
    to_chips(M_AG, lambda o: m_fin.at[c, my_rows], m_fin.at[c, my_rows])

    arrived(d_c.at[pl.ds(0, NA - 1)], D_C)
    for k in range(NA):
        i, j = k // 4, k % 4
        rows, cols = pl.ds(32 * i, 32), pl.ds(128 * j, 128)
        grad = d_c[k].astype(F32) / total
        ndown[rows, cols] = down[rows, cols] - rate_down * grad
    l32[...] = dot(ndown[...].astype(BF), dec[...], 1, 1)
    l_send[...] = l32[pl.ds(pl.multiple_of(oc * 32, 32), 32), :].astype(BF)
    remote(l_send, l_prec, L_PAIR, pair).start()
    nd_out[...] = two_rows(ndown, d // 4, 2 * (d % 4))
    cp_nd = load(nd_out, nd_h, O_ND)
    arrived(l_prec, L_PAIR)
    l_all[q] = (l32[pl.ds(pl.multiple_of(c * 32, 32), 32), :] + l_prec[...].astype(F32)).astype(BF)
    to_chips(L_ALL, lambda o: l_all.at[q], l_all.at[q])

    arrived(u_b.at[pl.ds(0, NB - 1)], U_B)
    u_fin[c, q] = total_of(u_b).astype(BF)
    to_chips(U_AG, lambda o: u_fin.at[c, q], u_fin.at[c, q])

    arrived(m_fin.at[c, pl.ds(0, 448)], M_AG)
    remote(m_fin.at[c], m_fin.at[c], M_PAIR2, pair).start()

    arrived(u_fin.at[c, pl.ds(0, NC - 1)], U_AG)
    remote(u_fin.at[c], u_fin.at[c], U_PAIR2, pair).start()

    arrived(m_fin.at[oc], M_PAIR2)
    cp_m = load(m_fin, m_h, O_M)

    arrived(u_fin.at[oc], U_PAIR2)
    for i in range(2):
        for j in range(NC):
            rows, cols = pl.ds(32 * i, 32), pl.ds(128 * j, 128)
            grad = u_fin[i, j].astype(F32) / total
            upt[rows, cols] = upt[rows, cols] - rate_up * grad
    nupt16[...] = upt[...].astype(BF)
    cp_nut = load(nupt16, nut_h, O_NUT)
    nup[...] = upt[...].T
    nu_out[...] = two_rows(nup, d * 4 + t // 4, 2 * (t % 4))
    cp_nu = load(nu_out, nu_h, O_NU)

    half = pl.ds(pl.multiple_of(c * 32, 32), 32)
    arrived(l_all.at[pl.ds(0, NC - 1)], L_ALL)
    l_fin[half, :] = total_of(l_all).astype(BF)
    remote(l_fin.at[half], l_fin.at[half], L_PAIR2, pair).start()
    arrived(l_fin.at[half], L_PAIR2)
    cp_ld = load(l_fin, ld_h, O_LD)

    m_part = m_fin.at[c, pl.ds(0, 448)]
    for ref, i in (
        (td_send.at[pl.ds(0, NA - 1)], D_A), (d_b.at[pl.ds(0, NB - 1)], D_B),
        (d_c.at[pl.ds(0, NA - 1)], D_C), (u_send, U_PAIR), (u_rs.at[pl.ds(0, NC - 1)], U_RS),
        (u_a.at[pl.ds(0, NA - 1)], U_A), (u_b.at[pl.ds(0, NB - 1)], U_B),
        (u_fin.at[c, pl.ds(0, NC - 1)], U_AG), (u_fin.at[c], U_PAIR2), (m_send, M_PAIR),
        (m_rs.at[pl.ds(0, NC - 1)], M_RS), (m_part, M_AG), (m_fin.at[c], M_PAIR2),
        (l_send, L_PAIR), (l_all.at[pl.ds(0, NC - 1)], L_ALL), (l_fin.at[half], L_PAIR2),
    ):
        sent(ref, i)
    for cp in (cp_ga, cp_nd, cp_m, cp_nut, cp_nu, cp_ld):
        cp.wait()


def finish_kernel(m_ref, ld_ref, nut_ref, ga_ref, nd_ref, nu_ref, dec_h, ga_h, nd_h, nu_h, dec_v, sem):
    small = [
        pltpu.make_async_copy(ref, out, sem.at[4 + i])
        for i, (ref, out) in enumerate(((ga_ref, ga_h), (nd_ref, nd_h), (nu_ref, nu_h)))
    ]
    for cp in small:
        cp.start()
    parts = []
    for r in range(4):
        rows = slice(128 * r, 128 * r + 128)
        corr = dot(ld_ref[:, rows], nut_ref[...], 0, 0)
        for h in range(2):
            cols = slice(512 * h, 512 * h + 512)
            dec_v[rows, cols] = (m_ref[h, rows, :].astype(F32) + corr[:, cols]).astype(BF)
        cp = pltpu.make_async_copy(dec_v.at[rows], dec_h.at[rows], sem.at[r])
        cp.start()
        parts.append(cp)
    for cp in parts + small:
        cp.wait()


def body(learn_acts, cotangent, base_weight, down_factor, up_factor, decode_acts):
    any_ = pl.BlockSpec(memory_space=pl.ANY)
    hbm = pl.BlockSpec(memory_space=pltpu.HBM)
    vmem = pl.BlockSpec(memory_space=pltpu.VMEM)
    V = pltpu.VMEM
    sds = jax.ShapeDtypeStruct
    ga, nd, nu, nut, ld, m = pl.pallas_call(
        comm_kernel,
        out_shape=(
            sds((512, 512), BF), sds((2, 512), F32), sds((2, 64), F32),
            sds((64, 1024), BF), sds((64, 512), BF), sds((2, 512, 512), BF),
        ),
        in_specs=[hbm] * 6,
        out_specs=(any_,) * 6,
        scratch_shapes=[
            V((512, 512), BF), V((512, 1024), BF), V((512, 1024), BF), V((64, 512), F32),
            V((512, 512), BF), V((512, 512), BF),
            V((512, 64), BF), V((NA, 32, 128), BF), V((NA, 32, 128), BF), V((NB, 32, 128), BF),
            V((NA, 32, 128), BF), V((64, 512), F32), V((2, 512), F32),
            V((2, NC, 32, 128), F32), V((NC, 32, 128), BF), V((NC, 32, 128), BF),
            V((NC, 32, 128), BF), V((NC, 32, 128), BF), V((NA, 32, 128), BF), V((NB, 32, 128), BF),
            V((2, NC, 32, 128), BF), V((64, 1024), F32), V((64, 1024), BF), V((1024, 64), F32),
            V((2, 64), F32),
            V((512, 512), BF), V((512, 512), F32), V((512, 512), BF), V((NC, 64, 512), BF),
            V((NC, 64, 512), BF), V((2, 512, 512), BF),
            V((64, 512), F32), V((32, 512), BF), V((32, 512), BF), V((NC, 32, 512), BF),
            V((64, 512), BF),
            pltpu.SemaphoreType.DMA((16,)), pltpu.SemaphoreType.DMA((16,)),
            pltpu.SemaphoreType.DMA((12,)),
        ],
        compiler_params=pltpu.CompilerParams(
            collective_id=0, has_side_effects=True, vmem_limit_bytes=48 * 1024 * 1024
        ),
        name="adapter_step",
    )(*(
        pltpu.with_memory_space_constraint(arg, pltpu.HBM)
        for arg in (
            learn_acts, cotangent, base_weight, down_factor, up_factor.T, decode_acts
        )
    ))
    decoded, ga, nd, nu = pl.pallas_call(
        finish_kernel,
        out_shape=(
            sds((512, 1024), BF), sds((512, 512), BF), sds((2, 512), F32), sds((2, 64), F32),
        ),
        in_specs=[vmem] * 6,
        out_specs=(hbm,) * 4,
        scratch_shapes=[V((512, 1024), BF), pltpu.SemaphoreType.DMA((7,))],
        compiler_params=pltpu.CompilerParams(vmem_limit_bytes=16 * 1024 * 1024),
        name="finish",
    )(m, ld, nut, ga, nd, nu)
    return (ga, nd, nu, decoded)


def solution(mesh):
    in_specs = (
        P("dp", "tensor"),
        P("dp", None),
        P("tensor", None),
        P(None, "tensor"),
        P(),
        P("dp", "tensor"),
    )
    out_specs = (P("dp", "tensor"), P("dp", "tensor"), P(("dp", "tensor"), None), P("dp", None))
    return jax.shard_map(body, mesh=mesh, in_specs=in_specs, out_specs=out_specs, check_vma=False)
```

```python
import jax
import jax.numpy as jnp
from jax import lax
from jax.experimental import pallas as pl
from jax.experimental.pallas import tpu as pltpu
from jax.sharding import PartitionSpec as P

rate_down = 0.2
rate_up = 3.0

NZ = 16
GZ = 4
NA = 8
NB = 4
NO = 4
NC = 8

BF = jnp.bfloat16
F32 = jnp.float32

(D_A, D_B, D_C, U_PAIR, U_RS, U_A, U_B, U_AG, U_PAIR2,
 M_PAIR, M_RS, M_AG, M_PAIR2, L_PAIR, L_ALL, L_PAIR2) = range(16)
(I_COT, I_UP, I_LEARN, I_DOWN, I_DEC, I_BASE,
 O_GA, O_ND, O_NU, O_NUT, O_LD, O_M) = range(12)


def dot(a, b, ca, cb):
    return lax.dot_general(a, b, (((ca,), (cb,)), ((), ())), preferred_element_type=F32)


def comm_kernel(
    learn_h, cot_h, base_h, down_h, up_h, dec_h,
    ga_h, nd_h, nu_h, nut_h, ld_h, m_h,
    learn, cot, base, down, dec, ga,
    lowout, td_send, d_a, d_b, d_c, ndown, nd_out,
    g32, u_send, u_prec, u_sum, u_rs, u_a, u_b, u_fin, upt, nupt16, nup, nu_out,
    m_send, m_keep, m_prec, m_sum, m_rs, m_fin,
    l32, l_send, l_prec, l_all, l_fin,
    ssem, rsem, rfar, lsem,
):
    d = lax.axis_index("dp")
    t = lax.axis_index("tensor")
    x = d // NZ
    z = d % NZ
    zb = z // GZ
    za = z % GZ
    a = x * GZ + za
    q = t // 2
    c = t % 2
    oc = 1 - c
    total = 16384.0

    def load(src, dst, i):
        cp = pltpu.make_async_copy(src, dst, lsem.at[i])
        cp.start()
        return cp

    cp_cot = load(cot_h, cot, I_COT)
    cp_up = load(up_h, upt, I_UP)
    cp_learn = load(learn_h, learn, I_LEARN)
    cp_down = load(down_h, down, I_DOWN)
    cp_dec = load(dec_h, dec, I_DEC)
    cp_base = load(base_h, base, I_BASE)

    owner = jnp.logical_or(za == 1, za == 2)
    mine = x * 2 + jnp.where(zb < 2, za - 1, 2 - za)

    def near(k):
        other = (a + k) % NA
        return other, {"dp": (other // GZ) * NZ + zb * GZ + other % GZ, "tensor": t}

    def owner_of(o):
        at = jnp.where(zb < 2, 1 + o % 2, 2 - o % 2)
        return (o // 2) * GZ + at, {"dp": (o // 2) * NZ + zb * GZ + at, "tensor": t}

    def column(group, at):
        return {"dp": x * NZ + group * GZ + at, "tensor": t}

    def far_down(k):
        return column(k, jnp.where((zb < 2) == (k < 2), za, GZ - 1 - za))

    def far_up(k):
        opposite = jnp.logical_or(zb == k + 2, zb == k - 2)
        return column(k, jnp.where(opposite, GZ - 1 - za, za))

    def chip(k):
        other = (q + k) % NC
        return other, {"dp": d, "tensor": other * 2 + c}

    pair = {"dp": d, "tensor": q * 2 + oc}

    barrier = pltpu.get_barrier_semaphore()

    def greet(dev):
        pl.semaphore_signal(barrier, inc=1, device_id=dev, device_id_type=pl.DeviceIdType.MESH)

    def hello_near(k, _):
        greet(near(k)[1])
        return 0

    def hello_chip(k, _):
        greet(chip(k)[1])
        return 0

    lax.fori_loop(1, NA, hello_near, 0)
    lax.fori_loop(1, NC, hello_chip, 0)
    greet(pair)
    for k in range(1, NB):
        @pl.when(zb < k)
        def _():
            greet(column(k, za))
            greet(column(k, GZ - 1 - za))

    def remote(src, dst, i, dev):
        return pltpu.make_async_remote_copy(
            src_ref=src, dst_ref=dst, send_sem=ssem.at[i], recv_sem=rsem.at[i],
            device_id=dev, device_id_type=pl.DeviceIdType.MESH,
        )

    def arrived(ref, i):
        remote(ref, ref, i, pair).wait_recv()

    def sent(ref, i):
        remote(ref, ref, i, pair).wait_send()

    def to_near(i, src, dst):
        def step(k, _):
            other, dev = near(k)
            remote(src(other), dst, i, dev).start()
            return 0
        lax.fori_loop(1, NA, step, 0)

    def send_far(i, dev, buf, k):
        pltpu.make_async_remote_copy(
            src_ref=buf.at[zb], dst_ref=buf.at[zb], send_sem=ssem.at[i],
            recv_sem=rfar.at[i, zb], device_id=dev(k), device_id_type=pl.DeviceIdType.MESH,
        ).start()

    def far_arrived(i, buf, k):
        pltpu.make_async_remote_copy(
            src_ref=buf.at[k], dst_ref=buf.at[k], send_sem=ssem.at[i],
            recv_sem=rfar.at[i, k], device_id=pair, device_id_type=pl.DeviceIdType.MESH,
        ).wait_recv()

    def far_down_first(i, dev, buf):
        for k in range(NB - 1):
            @pl.when(k < zb)
            def _():
                send_far(i, dev, buf, k)

    def far_rest(i, dev, buf):
        for k in range(1, NB):
            @pl.when(k > zb)
            def _():
                far_arrived(i, buf, k)
                send_far(i, dev, buf, k)
        for k in range(NB - 1):
            @pl.when(k < zb)
            def _():
                far_arrived(i, buf, k)

    def to_chips(i, src, dst):
        def step(k, _):
            other, dev = chip(k)
            remote(src(other), dst, i, dev).start()
            return 0
        lax.fori_loop(1, NC, step, 0)

    def total_of(ref):
        acc = ref[0].astype(F32)
        for k in range(1, ref.shape[0]):
            acc = acc + ref[k].astype(F32)
        return acc

    def two_rows(ref, block, first):
        rows = ref[pl.ds(pl.multiple_of(block * 8, 8), 8), :]
        at = lax.broadcasted_iota(jnp.int32, rows.shape, 0)
        picked = [
            jnp.sum(jnp.where(at == first + k, rows, 0.0), axis=0, keepdims=True) for k in range(2)
        ]
        return jnp.concatenate(picked, axis=0)

    cp_cot.wait()
    cp_up.wait()
    lowout[...] = dot(cot[...], upt[...].astype(BF), 1, 1).astype(BF)
    cp_learn.wait()
    term = dot(lowout[...], learn[...], 0, 0).astype(BF)
    for k in range(NO):
        i, j = k // 2, k % 2
        td_send[k] = term[32 * i:32 * i + 32, 256 * j:256 * j + 256]

    cp_down.wait()
    down16 = down[...].astype(BF)
    low_in = dot(down16, learn[...], 1, 1).astype(BF)
    term_up = dot(low_in, cot[...], 1, 0)
    for i in range(2):
        for j in range(NC):
            g32[i, j] = term_up[32 * i:32 * i + 32, 128 * j:128 * j + 128]
    u_send[...] = g32[oc].astype(BF)

    pl.semaphore_wait(barrier, (NA - 1) + (NC - 1) + 1 + 2 * zb)

    def to_owner(o, _):
        place, dev = owner_of(o)

        @pl.when(place != a)
        def _():
            remote(td_send.at[o], d_a.at[a], D_A, dev).start()
        return 0

    lax.fori_loop(0, NO, to_owner, 0)
    remote(u_send, u_prec, U_PAIR, pair).start()

    @pl.when(owner)
    def _():
        d_a[a] = td_send[mine]

    cp_dec.wait()
    cp_base.wait()

    def other_half(r, _):
        rows = pl.ds(pl.multiple_of(r * 128, 128), 128)
        cols = pl.ds(pl.multiple_of(oc * 512, 512), 512)
        m_send[rows, :] = dot(dec[rows, :], base[:, cols], 1, 0).astype(BF)
        return 0

    def own_half(r, _):
        rows = pl.ds(pl.multiple_of(r * 128, 128), 128)
        cols = pl.ds(pl.multiple_of(c * 512, 512), 512)
        m_keep[rows, :] = dot(dec[rows, :], base[:, cols], 1, 0)
        return 0

    lax.fori_loop(0, 4, other_half, 0)
    remote(m_send, m_prec, M_PAIR, pair).start()

    arrived(u_prec, U_PAIR)
    u_sum[...] = (g32[c] + u_prec[...].astype(F32)).astype(BF)
    u_rs[q] = u_sum[q]
    to_chips(U_RS, lambda o: u_sum.at[o], u_rs.at[q])

    lax.fori_loop(0, 4, own_half, 0)
    arrived(m_prec, M_PAIR)

    def add_half(r, _):
        rows = pl.ds(pl.multiple_of(r * 64, 64), 64)
        m_sum[r] = (m_keep[rows, :] + m_prec[rows, :].astype(F32)).astype(BF)
        return 0

    lax.fori_loop(0, NC, add_half, 0)
    m_rs[q] = m_sum[q]

    to_chips(M_RS, lambda o: m_sum.at[o], m_rs.at[q])

    @pl.when(owner)
    def _():
        arrived(d_a.at[pl.ds(0, NA - 1)], D_A)
        d_b[zb] = total_of(d_a).astype(BF)
        far_down_first(D_B, far_down, d_b)

    def acts(r, _):
        rows = pl.ds(pl.multiple_of(r * 128, 128), 128)
        ga[rows, :] = (
            dot(cot[rows, :], base[...], 1, 1) + dot(lowout[rows, :], down[...].astype(BF), 1, 0)
        ).astype(BF)
        return 0

    lax.fori_loop(0, 4, acts, 0)
    cp_ga = load(ga, ga_h, O_GA)

    arrived(u_rs.at[pl.ds(0, NC - 1)], U_RS)
    u_a[a] = total_of(u_rs).astype(BF)
    to_near(U_A, lambda o: u_a.at[a], u_a.at[a])

    arrived(u_a.at[pl.ds(0, NA - 1)], U_A)
    u_b[zb] = total_of(u_a).astype(BF)
    far_down_first(U_B, far_up, u_b)

    my_rows = pl.ds(pl.multiple_of(q * 64, 64), 64)
    arrived(m_rs.at[pl.ds(0, NC - 1)], M_RS)
    m_fin[c, my_rows, :] = total_of(m_rs).astype(BF)
    to_chips(M_AG, lambda o: m_fin.at[c, my_rows], m_fin.at[c, my_rows])

    @pl.when(owner)
    def _():
        far_rest(D_B, far_down, d_b)
        d_c[mine] = total_of(d_b).astype(BF)
        to_near(D_C, lambda o: d_c.at[mine], d_c.at[mine])

    arrived(m_fin.at[c, pl.ds(0, 448)], M_AG)
    remote(m_fin.at[c], m_fin.at[c], M_PAIR2, pair).start()

    @pl.when(owner)
    def _():
        arrived(d_c.at[pl.ds(0, NO - 1)], D_C)

    @pl.when(jnp.logical_not(owner))
    def _():
        arrived(d_c, D_C)

    for k in range(NO):
        i, j = k // 2, k % 2
        rows, cols = pl.ds(32 * i, 32), pl.ds(256 * j, 256)
        grad = d_c[k].astype(F32) / total
        ndown[rows, cols] = down[rows, cols] - rate_down * grad
    l32[...] = dot(ndown[...].astype(BF), dec[...], 1, 1)
    l_send[...] = l32[pl.ds(pl.multiple_of(oc * 32, 32), 32), :].astype(BF)
    remote(l_send, l_prec, L_PAIR, pair).start()
    nd_out[...] = two_rows(ndown, d // 4, 2 * (d % 4))
    cp_nd = load(nd_out, nd_h, O_ND)
    arrived(l_prec, L_PAIR)
    l_all[q] = (l32[pl.ds(pl.multiple_of(c * 32, 32), 32), :] + l_prec[...].astype(F32)).astype(BF)
    to_chips(L_ALL, lambda o: l_all.at[q], l_all.at[q])

    far_rest(U_B, far_up, u_b)
    u_fin[c, q] = total_of(u_b).astype(BF)
    to_chips(U_AG, lambda o: u_fin.at[c, q], u_fin.at[c, q])

    arrived(u_fin.at[c, pl.ds(0, NC - 1)], U_AG)
    remote(u_fin.at[c], u_fin.at[c], U_PAIR2, pair).start()

    arrived(m_fin.at[oc], M_PAIR2)
    cp_m = load(m_fin, m_h, O_M)

    arrived(u_fin.at[oc], U_PAIR2)
    for i in range(2):
        for j in range(NC):
            rows, cols = pl.ds(32 * i, 32), pl.ds(128 * j, 128)
            grad = u_fin[i, j].astype(F32) / total
            upt[rows, cols] = upt[rows, cols] - rate_up * grad
    nupt16[...] = upt[...].astype(BF)
    cp_nut = load(nupt16, nut_h, O_NUT)
    first = d * 32 + t * 2
    nup[...] = upt[:, pl.ds(pl.multiple_of(first // 128 * 128, 128), 128)].T
    nu_out[...] = two_rows(nup, first % 128 // 8, first % 8)
    cp_nu = load(nu_out, nu_h, O_NU)

    half = pl.ds(pl.multiple_of(c * 32, 32), 32)
    arrived(l_all.at[pl.ds(0, NC - 1)], L_ALL)
    l_fin[half, :] = total_of(l_all).astype(BF)
    remote(l_fin.at[half], l_fin.at[half], L_PAIR2, pair).start()
    arrived(l_fin.at[half], L_PAIR2)
    cp_ld = load(l_fin, ld_h, O_LD)

    m_part = m_fin.at[c, pl.ds(0, 448)]
    for ref, i in (
        (u_send, U_PAIR), (u_rs.at[pl.ds(0, NC - 1)], U_RS),
        (u_a.at[pl.ds(0, NA - 1)], U_A), (u_b.at[pl.ds(0, NB - 1)], U_B),
        (u_fin.at[c, pl.ds(0, NC - 1)], U_AG), (u_fin.at[c], U_PAIR2), (m_send, M_PAIR),
        (m_rs.at[pl.ds(0, NC - 1)], M_RS), (m_part, M_AG), (m_fin.at[c], M_PAIR2),
        (l_send, L_PAIR), (l_all.at[pl.ds(0, NC - 1)], L_ALL), (l_fin.at[half], L_PAIR2),
    ):
        sent(ref, i)

    @pl.when(owner)
    def _():
        sent(td_send.at[pl.ds(0, NO - 1)], D_A)
        sent(d_b.at[pl.ds(0, NB - 1)], D_B)
        sent(d_a.at[pl.ds(0, NA - 1)], D_C)

    @pl.when(jnp.logical_not(owner))
    def _():
        sent(td_send, D_A)

    for cp in (cp_ga, cp_nd, cp_m, cp_nut, cp_nu, cp_ld):
        cp.wait()


def finish_kernel(m_ref, ld_ref, nut_ref, ga_ref, nd_ref, nu_ref, dec_h, ga_h, nd_h, nu_h, dec_v, sem):
    small = [
        pltpu.make_async_copy(ref, out, sem.at[4 + i])
        for i, (ref, out) in enumerate(((ga_ref, ga_h), (nd_ref, nd_h), (nu_ref, nu_h)))
    ]
    for cp in small:
        cp.start()
    parts = []
    for r in range(4):
        rows = slice(128 * r, 128 * r + 128)
        corr = dot(ld_ref[:, rows], nut_ref[...], 0, 0)
        for h in range(2):
            cols = slice(512 * h, 512 * h + 512)
            dec_v[rows, cols] = (m_ref[h, rows, :].astype(F32) + corr[:, cols]).astype(BF)
        cp = pltpu.make_async_copy(dec_v.at[rows], dec_h.at[rows], sem.at[r])
        cp.start()
        parts.append(cp)
    for cp in parts + small:
        cp.wait()


def body(learn_acts, cotangent, base_weight, down_factor, up_factor, decode_acts):
    any_ = pl.BlockSpec(memory_space=pl.ANY)
    hbm = pl.BlockSpec(memory_space=pltpu.HBM)
    vmem = pl.BlockSpec(memory_space=pltpu.VMEM)
    V = pltpu.VMEM
    sds = jax.ShapeDtypeStruct
    ga, nd, nu, nut, ld, m = pl.pallas_call(
        comm_kernel,
        out_shape=(
            sds((512, 512), BF), sds((2, 512), F32), sds((2, 64), F32),
            sds((64, 1024), BF), sds((64, 512), BF), sds((2, 512, 512), BF),
        ),
        in_specs=[hbm] * 6,
        out_specs=(any_,) * 6,
        scratch_shapes=[
            V((512, 512), BF), V((512, 1024), BF), V((512, 1024), BF), V((64, 512), F32),
            V((512, 512), BF), V((512, 512), BF),
            V((512, 64), BF), V((NO, 32, 256), BF), V((NA, 32, 256), BF), V((NB, 32, 256), BF),
            V((NO, 32, 256), BF), V((64, 512), F32), V((2, 512), F32),
            V((2, NC, 32, 128), F32), V((NC, 32, 128), BF), V((NC, 32, 128), BF),
            V((NC, 32, 128), BF), V((NC, 32, 128), BF), V((NA, 32, 128), BF), V((NB, 32, 128), BF),
            V((2, NC, 32, 128), BF), V((64, 1024), F32), V((64, 1024), BF), V((128, 64), F32),
            V((2, 64), F32),
            V((512, 512), BF), V((512, 512), F32), V((512, 512), BF), V((NC, 64, 512), BF),
            V((NC, 64, 512), BF), V((2, 512, 512), BF),
            V((64, 512), F32), V((32, 512), BF), V((32, 512), BF), V((NC, 32, 512), BF),
            V((64, 512), BF),
            pltpu.SemaphoreType.DMA((16,)), pltpu.SemaphoreType.DMA((16,)),
            pltpu.SemaphoreType.DMA((16, NB)),
            pltpu.SemaphoreType.DMA((12,)),
        ],
        compiler_params=pltpu.CompilerParams(
            collective_id=0, has_side_effects=True, vmem_limit_bytes=48 * 1024 * 1024
        ),
        name="adapter_step",
    )(*(
        pltpu.with_memory_space_constraint(arg, pltpu.HBM)
        for arg in (
            learn_acts, cotangent, base_weight, down_factor, up_factor.T, decode_acts
        )
    ))
    decoded, ga, nd, nu = pl.pallas_call(
        finish_kernel,
        out_shape=(
            sds((512, 1024), BF), sds((512, 512), BF), sds((2, 512), F32), sds((2, 64), F32),
        ),
        in_specs=[vmem] * 6,
        out_specs=(hbm,) * 4,
        scratch_shapes=[V((512, 1024), BF), pltpu.SemaphoreType.DMA((7,))],
        compiler_params=pltpu.CompilerParams(vmem_limit_bytes=16 * 1024 * 1024),
        name="finish",
    )(m, ld, nut, ga, nd, nu)
    return (ga, nd, nu, decoded)


def solution(mesh):
    in_specs = (
        P("dp", "tensor"),
        P("dp", None),
        P("tensor", None),
        P(None, "tensor"),
        P(),
        P("dp", "tensor"),
    )
    out_specs = (P("dp", "tensor"), P("dp", "tensor"), P(("dp", "tensor"), None), P("dp", None))
    return jax.shard_map(body, mesh=mesh, in_specs=in_specs, out_specs=out_specs, check_vma=False)
```

```python
import jax
import jax.numpy as jnp
from jax import lax
from jax.experimental import pallas as pl
from jax.experimental.pallas import tpu as pltpu
from jax.sharding import PartitionSpec as P

rate_down = 0.2
rate_up = 3.0

NZ = 16
GZ = 4
NA = 8
NB = 4
NO = 4
NC = 8

BF = jnp.bfloat16
F32 = jnp.float32

(D_A, D_B, D_C, U_PAIR, U_RS, U_A, U_B, U_AG, U_PAIR2,
 M_PAIR, M_RS, M_AG, M_PAIR2, L_PAIR, L_ALL, L_PAIR2) = range(16)
(I_COT, I_UP, I_LEARN, I_DOWN, I_DEC, I_BASE, O_M) = range(7)


def dot(a, b, ca, cb):
    return lax.dot_general(a, b, (((ca,), (cb,)), ((), ())), preferred_element_type=F32)


def comm_kernel(
    learn_h, cot_h, base_h, down_h, up_h, dec_h,
    ga, nd_out, nu_out, nupt16, l_fin, m_h,
    learn, cot, base, down, dec,
    lowout, td_send, d_a, d_b, d_c, ndown,
    g32, u_send, u_prec, u_sum, u_rs, u_a, u_b, u_fin, upt, nup,
    m_send, m_keep, m_prec, m_sum, m_rs, m_fin,
    l32, l_send, l_prec, l_all,
    ssem, rsem, rfar, lsem, entered,
):
    d = lax.axis_index("dp")
    t = lax.axis_index("tensor")
    x = d // NZ
    z = d % NZ
    zb = z // GZ
    za = z % GZ
    a = x * GZ + za
    q = t // 2
    c = t % 2
    oc = 1 - c
    total = 16384.0

    def load(src, dst, i):
        cp = pltpu.make_async_copy(src, dst, lsem.at[i])
        cp.start()
        return cp

    cp_down = load(down_h, down, I_DOWN)
    cp_learn = load(learn_h, learn, I_LEARN)
    cp_up = load(up_h, upt, I_UP)
    cp_cot = load(cot_h, cot, I_COT)
    cp_dec = load(dec_h, dec, I_DEC)
    cp_base = load(base_h, base, I_BASE)

    owner = jnp.logical_or(za == 1, za == 2)
    mine = x * 2 + jnp.where(zb < 2, za - 1, 2 - za)

    def near(k):
        other = (a + k) % NA
        return other, {"dp": (other // GZ) * NZ + zb * GZ + other % GZ, "tensor": t}

    def owner_of(o):
        at = jnp.where(zb < 2, 1 + o % 2, 2 - o % 2)
        return (o // 2) * GZ + at, {"dp": (o // 2) * NZ + zb * GZ + at, "tensor": t}

    def column(group, at):
        return {"dp": x * NZ + group * GZ + at, "tensor": t}

    def far_down(k):
        return column(k, jnp.where((zb < 2) == (k < 2), za, GZ - 1 - za))

    def far_up(k):
        opposite = jnp.logical_or(zb == k + 2, zb == k - 2)
        return column(k, jnp.where(opposite, GZ - 1 - za, za))

    def chip(k):
        other = (q + k) % NC
        return other, {"dp": d, "tensor": other * 2 + c}

    pair = {"dp": d, "tensor": q * 2 + oc}

    barrier = pltpu.get_barrier_semaphore()

    def greet(dev):
        pl.semaphore_signal(barrier, inc=1, device_id=dev, device_id_type=pl.DeviceIdType.MESH)

    def hello_near(k, _):
        greet(near(k)[1])
        return 0

    def hello_chip(k, _):
        greet(chip(k)[1])
        return 0

    lax.fori_loop(1, NA, hello_near, 0)
    lax.fori_loop(1, NC, hello_chip, 0)
    greet(pair)
    for k in range(1, NB):
        @pl.when(zb < k)
        def _():
            greet(column(k, za))
            greet(column(k, GZ - 1 - za))

    def remote(src, dst, i, dev):
        return pltpu.make_async_remote_copy(
            src_ref=src, dst_ref=dst, send_sem=ssem.at[i], recv_sem=rsem.at[i],
            device_id=dev, device_id_type=pl.DeviceIdType.MESH,
        )

    def arrived(ref, i):
        remote(ref, ref, i, pair).wait_recv()

    def sent(ref, i):
        remote(ref, ref, i, pair).wait_send()

    def to_near(i, src, dst):
        def step(k, _):
            other, dev = near(k)
            remote(src(other), dst, i, dev).start()
            return 0
        lax.fori_loop(1, NA, step, 0)

    def send_far(i, dev, buf, k):
        pltpu.make_async_remote_copy(
            src_ref=buf.at[zb], dst_ref=buf.at[zb], send_sem=ssem.at[i],
            recv_sem=rfar.at[i, zb], device_id=dev(k), device_id_type=pl.DeviceIdType.MESH,
        ).start()

    def far_arrived(i, buf, k):
        pltpu.make_async_remote_copy(
            src_ref=buf.at[k], dst_ref=buf.at[k], send_sem=ssem.at[i],
            recv_sem=rfar.at[i, k], device_id=pair, device_id_type=pl.DeviceIdType.MESH,
        ).wait_recv()

    def far_send(i, dev, buf, wanted):
        for step in (1, 3, 2):
            k = (zb + step) % NB

            @pl.when(k > zb if wanted == "higher" else k < zb)
            def _():
                send_far(i, dev, buf, k)

    def far_wait(i, buf):
        for step in range(1, NB):
            far_arrived(i, buf, (zb + step) % NB)

    def to_chips(i, src, dst):
        def step(k, _):
            other, dev = chip(k)
            remote(src(other), dst, i, dev).start()
            return 0
        lax.fori_loop(1, NC, step, 0)

    def total_of(ref):
        acc = ref[0].astype(F32)
        for k in range(1, ref.shape[0]):
            acc = acc + ref[k].astype(F32)
        return acc

    def two_rows(ref, block, first):
        rows = ref[pl.ds(pl.multiple_of(block * 8, 8), 8), :]
        at = lax.broadcasted_iota(jnp.int32, rows.shape, 0)
        picked = [
            jnp.sum(jnp.where(at == first + k, rows, 0.0), axis=0, keepdims=True) for k in range(2)
        ]
        return jnp.concatenate(picked, axis=0)

    cp_down.wait()
    cp_learn.wait()
    low_in = dot(down[...].astype(BF), learn[...], 1, 1).astype(BF)
    cp_up.wait()
    cp_cot.wait()
    lowout[...] = dot(cot[...], upt[...].astype(BF), 1, 1).astype(BF)
    term = dot(lowout[...], learn[...], 0, 0).astype(BF)
    for k in range(NO):
        i, j = k // 2, k % 2
        td_send[k] = term[32 * i:32 * i + 32, 256 * j:256 * j + 256]

    pl.semaphore_wait(barrier, (NA - 1) + (NC - 1) + 1 + 2 * zb)

    def to_owner(o, _):
        place, dev = owner_of(o)

        @pl.when(place != a)
        def _():
            remote(td_send.at[o], d_a.at[a], D_A, dev).start()
        return 0

    lax.fori_loop(0, NO, to_owner, 0)

    for k in range(NB - 1):
        @pl.when(k < zb)
        def _():
            for at in (za, GZ - 1 - za):
                pl.semaphore_signal(
                    entered, inc=1, device_id=column(k, at), device_id_type=pl.DeviceIdType.MESH
                )

    term_up = dot(low_in, cot[...], 1, 0)
    for i in range(2):
        for j in range(NC):
            g32[i, j] = term_up[32 * i:32 * i + 32, 128 * j:128 * j + 128]
    u_send[...] = g32[oc].astype(BF)
    remote(u_send, u_prec, U_PAIR, pair).start()

    @pl.when(owner)
    def _():
        d_a[a] = td_send[mine]

    cp_dec.wait()
    cp_base.wait()

    def other_half(r, _):
        to = pl.ds(pl.multiple_of(r * 256, 256), 256)
        cols = pl.ds(pl.multiple_of(oc * 512 + r * 256, 256), 256)
        m_send[:, to] = dot(dec[...], base[:, cols], 1, 0).astype(BF)
        return 0

    def own_half(r, _):
        to = pl.ds(pl.multiple_of(r * 256, 256), 256)
        cols = pl.ds(pl.multiple_of(c * 512 + r * 256, 256), 256)
        m_keep[:, to] = dot(dec[...], base[:, cols], 1, 0)
        return 0

    lax.fori_loop(0, 2, other_half, 0)
    remote(m_send, m_prec, M_PAIR, pair).start()

    arrived(u_prec, U_PAIR)
    u_sum[...] = (g32[c] + u_prec[...].astype(F32)).astype(BF)
    u_rs[q] = u_sum[q]
    to_chips(U_RS, lambda o: u_sum.at[o], u_rs.at[q])

    lax.fori_loop(0, 2, own_half, 0)
    arrived(m_prec, M_PAIR)

    def add_half(r, _):
        rows = pl.ds(pl.multiple_of(r * 64, 64), 64)
        m_sum[r] = (m_keep[rows, :] + m_prec[rows, :].astype(F32)).astype(BF)
        return 0

    lax.fori_loop(0, NC, add_half, 0)
    m_rs[q] = m_sum[q]

    to_chips(M_RS, lambda o: m_sum.at[o], m_rs.at[q])

    @pl.when(owner)
    def _():
        arrived(d_a.at[pl.ds(0, NA - 1)], D_A)
        d_b[zb] = total_of(d_a).astype(BF)
        far_send(D_B, far_down, d_b, "lower")

    arrived(u_rs.at[pl.ds(0, NC - 1)], U_RS)
    u_a[a] = total_of(u_rs).astype(BF)
    to_near(U_A, lambda o: u_a.at[a], u_a.at[a])

    arrived(u_a.at[pl.ds(0, NA - 1)], U_A)
    u_b[zb] = total_of(u_a).astype(BF)
    far_send(U_B, far_up, u_b, "lower")

    my_rows = pl.ds(pl.multiple_of(q * 64, 64), 64)
    arrived(m_rs.at[pl.ds(0, NC - 1)], M_RS)
    m_fin[c, my_rows, :] = total_of(m_rs).astype(BF)
    to_chips(M_AG, lambda o: m_fin.at[c, my_rows], m_fin.at[c, my_rows])

    @pl.when(zb < NB - 1)
    def _():
        pl.semaphore_wait(entered, 2 * (NB - 1 - zb))

    @pl.when(owner)
    def _():
        far_send(D_B, far_down, d_b, "higher")

    far_send(U_B, far_up, u_b, "higher")

    def acts(r, _):
        cols = pl.ds(pl.multiple_of(r * 256, 256), 256)
        ga[:, cols] = (
            dot(cot[...], base[cols, :], 1, 1) + dot(lowout[...], down[:, cols].astype(BF), 1, 0)
        ).astype(BF)
        return 0

    lax.fori_loop(0, 2, acts, 0)

    @pl.when(owner)
    def _():
        far_wait(D_B, d_b)
        d_c[mine] = total_of(d_b).astype(BF)
        to_near(D_C, lambda o: d_c.at[mine], d_c.at[mine])

    @pl.when(owner)
    def _():
        arrived(d_c.at[pl.ds(0, NO - 1)], D_C)

    @pl.when(jnp.logical_not(owner))
    def _():
        arrived(d_c, D_C)

    for k in range(NO):
        i, j = k // 2, k % 2
        rows, cols = pl.ds(32 * i, 32), pl.ds(256 * j, 256)
        grad = d_c[k].astype(F32) / total
        ndown[rows, cols] = down[rows, cols] - rate_down * grad
    l32[...] = dot(ndown[...].astype(BF), dec[...], 1, 1)
    l_send[...] = l32[pl.ds(pl.multiple_of(oc * 32, 32), 32), :].astype(BF)
    remote(l_send, l_prec, L_PAIR, pair).start()
    nd_out[...] = two_rows(ndown, d // 4, 2 * (d % 4))
    arrived(l_prec, L_PAIR)
    l_all[q] = (l32[pl.ds(pl.multiple_of(c * 32, 32), 32), :] + l_prec[...].astype(F32)).astype(BF)
    to_chips(L_ALL, lambda o: l_all.at[q], l_all.at[q])

    far_wait(U_B, u_b)
    u_fin[c, q] = total_of(u_b).astype(BF)
    to_chips(U_AG, lambda o: u_fin.at[c, q], u_fin.at[c, q])

    arrived(m_fin.at[c, pl.ds(0, 448)], M_AG)
    remote(m_fin.at[c], m_fin.at[c], M_PAIR2, pair).start()
    arrived(m_fin.at[oc], M_PAIR2)
    cp_m = load(m_fin, m_h, O_M)

    arrived(u_fin.at[c, pl.ds(0, NC - 1)], U_AG)
    remote(u_fin.at[c], u_fin.at[c], U_PAIR2, pair).start()

    half = pl.ds(pl.multiple_of(c * 32, 32), 32)
    arrived(l_all.at[pl.ds(0, NC - 1)], L_ALL)
    l_fin[half, :] = total_of(l_all).astype(BF)
    remote(l_fin.at[half], l_fin.at[half], L_PAIR2, pair).start()

    arrived(u_fin.at[oc], U_PAIR2)
    for i in range(2):
        for j in range(NC):
            rows, cols = pl.ds(32 * i, 32), pl.ds(128 * j, 128)
            grad = u_fin[i, j].astype(F32) / total
            new = upt[rows, cols] - rate_up * grad
            upt[rows, cols] = new
            nupt16[rows, cols] = new.astype(BF)
    first = d * 32 + t * 2
    nup[...] = upt[:, pl.ds(pl.multiple_of(first // 128 * 128, 128), 128)].T
    nu_out[...] = two_rows(nup, first % 128 // 8, first % 8)

    arrived(l_fin.at[half], L_PAIR2)

    m_part = m_fin.at[c, pl.ds(0, 448)]
    for ref, i in (
        (u_send, U_PAIR), (u_rs.at[pl.ds(0, NC - 1)], U_RS),
        (u_a.at[pl.ds(0, NA - 1)], U_A), (u_b.at[pl.ds(0, NB - 1)], U_B),
        (u_fin.at[c, pl.ds(0, NC - 1)], U_AG), (u_fin.at[c], U_PAIR2), (m_send, M_PAIR),
        (m_rs.at[pl.ds(0, NC - 1)], M_RS), (m_part, M_AG), (m_fin.at[c], M_PAIR2),
        (l_send, L_PAIR), (l_all.at[pl.ds(0, NC - 1)], L_ALL), (l_fin.at[half], L_PAIR2),
    ):
        sent(ref, i)

    @pl.when(owner)
    def _():
        sent(td_send.at[pl.ds(0, NO - 1)], D_A)
        sent(d_b.at[pl.ds(0, NB - 1)], D_B)
        sent(d_a.at[pl.ds(0, NA - 1)], D_C)

    @pl.when(jnp.logical_not(owner))
    def _():
        sent(td_send, D_A)

    cp_m.wait()


def finish_kernel(m_ref, ld_ref, nut_ref, ga_ref, nd_ref, nu_ref, dec_h, ga_h, nd_h, nu_h, dec_v, sem):
    small = [
        pltpu.make_async_copy(ref, out, sem.at[4 + i])
        for i, (ref, out) in enumerate(((ga_ref, ga_h), (nd_ref, nd_h), (nu_ref, nu_h)))
    ]
    for cp in small:
        cp.start()
    parts = []
    for r in range(4):
        rows = slice(128 * r, 128 * r + 128)
        corr = dot(ld_ref[:, rows], nut_ref[...], 0, 0)
        for h in range(2):
            cols = slice(512 * h, 512 * h + 512)
            dec_v[rows, cols] = (m_ref[h, rows, :].astype(F32) + corr[:, cols]).astype(BF)
        cp = pltpu.make_async_copy(dec_v.at[rows], dec_h.at[rows], sem.at[r])
        cp.start()
        parts.append(cp)
    for cp in parts + small:
        cp.wait()


def body(learn_acts, cotangent, base_weight, down_factor, up_factor, decode_acts):
    any_ = pl.BlockSpec(memory_space=pl.ANY)
    hbm = pl.BlockSpec(memory_space=pltpu.HBM)
    vmem = pl.BlockSpec(memory_space=pltpu.VMEM)
    V = pltpu.VMEM
    sds = jax.ShapeDtypeStruct
    ga, nd, nu, nut, ld, m = pl.pallas_call(
        comm_kernel,
        out_shape=(
            sds((512, 512), BF), sds((2, 512), F32), sds((2, 64), F32),
            sds((64, 1024), BF), sds((64, 512), BF), sds((2, 512, 512), BF),
        ),
        in_specs=[hbm] * 6,
        out_specs=(vmem,) * 5 + (any_,),
        scratch_shapes=[
            V((512, 512), BF), V((512, 1024), BF), V((512, 1024), BF), V((64, 512), F32),
            V((512, 512), BF),
            V((512, 64), BF), V((NO, 32, 256), BF), V((NA, 32, 256), BF), V((NB, 32, 256), BF),
            V((NO, 32, 256), BF), V((64, 512), F32),
            V((2, NC, 32, 128), F32), V((NC, 32, 128), BF), V((NC, 32, 128), BF),
            V((NC, 32, 128), BF), V((NC, 32, 128), BF), V((NA, 32, 128), BF), V((NB, 32, 128), BF),
            V((2, NC, 32, 128), BF), V((64, 1024), F32), V((128, 64), F32),
            V((512, 512), BF), V((512, 512), F32), V((512, 512), BF), V((NC, 64, 512), BF),
            V((NC, 64, 512), BF), V((2, 512, 512), BF),
            V((64, 512), F32), V((32, 512), BF), V((32, 512), BF), V((NC, 32, 512), BF),
            pltpu.SemaphoreType.DMA((16,)), pltpu.SemaphoreType.DMA((16,)),
            pltpu.SemaphoreType.DMA((16, NB)),
            pltpu.SemaphoreType.DMA((7,)), pltpu.SemaphoreType.REGULAR,
        ],
        compiler_params=pltpu.CompilerParams(
            collective_id=0, has_side_effects=True, vmem_limit_bytes=48 * 1024 * 1024
        ),
        name="adapter_step",
    )(*(
        pltpu.with_memory_space_constraint(arg, pltpu.HBM)
        for arg in (
            learn_acts, cotangent, base_weight, down_factor, up_factor.T, decode_acts
        )
    ))
    decoded, ga, nd, nu = pl.pallas_call(
        finish_kernel,
        out_shape=(
            sds((512, 1024), BF), sds((512, 512), BF), sds((2, 512), F32), sds((2, 64), F32),
        ),
        in_specs=[vmem] * 6,
        out_specs=(hbm,) * 4,
        scratch_shapes=[V((512, 1024), BF), pltpu.SemaphoreType.DMA((7,))],
        compiler_params=pltpu.CompilerParams(vmem_limit_bytes=16 * 1024 * 1024),
        name="finish",
    )(m, ld, nut, ga, nd, nu)
    return (ga, nd, nu, decoded)


def solution(mesh):
    in_specs = (
        P("dp", "tensor"),
        P("dp", None),
        P("tensor", None),
        P(None, "tensor"),
        P(),
        P("dp", "tensor"),
    )
    out_specs = (P("dp", "tensor"), P("dp", "tensor"), P(("dp", "tensor"), None), P("dp", None))
    return jax.shard_map(body, mesh=mesh, in_specs=in_specs, out_specs=out_specs, check_vma=False)
```

```python
import jax
import jax.numpy as jnp
from jax import lax
from jax.experimental import pallas as pl
from jax.experimental.pallas import tpu as pltpu
from jax.sharding import PartitionSpec as P

rate_down = 0.2
rate_up = 3.0

NZ = 16
GZ = 4
NA = 8
NB = 4
NO = 4
NC = 8
NW = 16

BF = jnp.bfloat16
F32 = jnp.float32

(D_A, D_B, D_C, U_PAIR, U_RS, U_A, U_B, U_AG, U_PAIR2,
 M_PAIR, M_RS, M_AG, M_PAIR2, DEC_PAIR, L_ALL, L_PAIR2, DOWN_PAIR, ND_PAIR) = range(18)
(I_COT, I_UP, I_LEARN, I_DOWN, I_DEC, I_BASE, O_M) = range(7)


def dot(a, b, ca, cb):
    return lax.dot_general(a, b, (((ca,), (cb,)), ((), ())), preferred_element_type=F32)


def comm_kernel(
    learn_h, cot_h, base_h, down_h, up_h, dec_h,
    ga, nd_out, nu_out, nupt16, l_fin, m_h,
    learn, cot, base, down, dec, dec_p, down_p,
    lowout, low_in, td_send, d_a, d_b, d_o, d_c, ndown, ndown_p, nd_send, nd_prec,
    u_send, u_prec, u_sum, u_rs, u_a, u_b, u_fin, upt, nup,
    m_send, m_keep, m_prec, m_sum, m_rs, m_fin, l_all,
    ssem, rsem, rfar, lsem, entered,
):
    d = lax.axis_index("dp")
    t = lax.axis_index("tensor")
    x = d // NZ
    z = d % NZ
    zb = z // GZ
    za = z % GZ
    a = x * GZ + za
    q = t // 2
    c = t % 2
    oc = 1 - c
    w = x * NC + q
    total = 16384.0

    def load(src, dst, i):
        cp = pltpu.make_async_copy(src, dst, lsem.at[i])
        cp.start()
        return cp

    cp_down = load(down_h, down, I_DOWN)
    cp_learn = load(learn_h, learn, I_LEARN)
    cp_up = load(up_h, upt, I_UP)
    cp_cot = load(cot_h, cot, I_COT)
    cp_dec = load(dec_h, dec, I_DEC)
    cp_base = load(base_h, base, I_BASE)

    owner = jnp.logical_or(za == 1, za == 2)
    mine = x * 2 + jnp.where(zb < 2, za - 1, 2 - za)

    def near(k):
        other = (a + k) % NA
        return other, {"dp": (other // GZ) * NZ + zb * GZ + other % GZ, "tensor": t}

    def near_core(k, core):
        return {"dp": near(k)[1]["dp"], "tensor": q * 2 + core}

    def owner_of(o):
        at = jnp.where(zb < 2, 1 + o % 2, 2 - o % 2)
        return (o // 2) * GZ + at, {"dp": (o // 2) * NZ + zb * GZ + at, "tensor": t}

    def column(group, at):
        return {"dp": x * NZ + group * GZ + at, "tensor": t}

    def far_down(k):
        return column(k, jnp.where((zb < 2) == (k < 2), za, GZ - 1 - za))

    def far_up(k):
        opposite = jnp.logical_or(zb == k + 2, zb == k - 2)
        return column(k, jnp.where(opposite, GZ - 1 - za, za))

    def wide(k):
        other = (w + k) % NW
        return other, {"dp": (other // NC) * NZ + z, "tensor": (other % NC) * 2 + c}

    def above(k):
        return {"dp": x * NZ + zb * GZ + (za + k) % GZ, "tensor": t}

    def chip(k):
        other = (q + k) % NC
        return other, {"dp": d, "tensor": other * 2 + c}

    pair = {"dp": d, "tensor": q * 2 + oc}

    barrier = pltpu.get_barrier_semaphore()

    def greet(dev):
        pl.semaphore_signal(barrier, inc=1, device_id=dev, device_id_type=pl.DeviceIdType.MESH)

    def hello_near(k, _):
        for core in range(2):
            greet(near_core(k, core))
        return 0

    def hello_wide(k, _):
        greet(wide(k)[1])
        return 0

    lax.fori_loop(1, NA, hello_near, 0)
    lax.fori_loop(1, NW, hello_wide, 0)
    greet(pair)
    for k in range(1, NB):
        @pl.when(zb < k)
        def _():
            greet(column(k, za))
            greet(column(k, GZ - 1 - za))

    def remote(src, dst, i, dev):
        return pltpu.make_async_remote_copy(
            src_ref=src, dst_ref=dst, send_sem=ssem.at[i], recv_sem=rsem.at[i],
            device_id=dev, device_id_type=pl.DeviceIdType.MESH,
        )

    def arrived(ref, i):
        remote(ref, ref, i, pair).wait_recv()

    def sent(ref, i):
        remote(ref, ref, i, pair).wait_send()

    def each(n, place, i, src, dst):
        def step(k, _):
            other, dev = place(k)
            remote(src(other), dst, i, dev).start()
            return 0
        lax.fori_loop(1, n, step, 0)

    def send_far(i, dev, buf, k):
        pltpu.make_async_remote_copy(
            src_ref=buf.at[zb], dst_ref=buf.at[zb], send_sem=ssem.at[i],
            recv_sem=rfar.at[i, zb], device_id=dev(k), device_id_type=pl.DeviceIdType.MESH,
        ).start()

    def far_arrived(i, buf, k):
        pltpu.make_async_remote_copy(
            src_ref=buf.at[k], dst_ref=buf.at[k], send_sem=ssem.at[i],
            recv_sem=rfar.at[i, k], device_id=pair, device_id_type=pl.DeviceIdType.MESH,
        ).wait_recv()

    def far_send(i, dev, buf, wanted):
        for step in (1, 3, 2):
            k = (zb + step) % NB

            @pl.when(k > zb if wanted == "higher" else k < zb)
            def _():
                send_far(i, dev, buf, k)

    def far_wait(i, buf):
        for step in range(1, NB):
            far_arrived(i, buf, (zb + step) % NB)

    def total_of(ref):
        acc = ref[0].astype(F32)
        for k in range(1, ref.shape[0]):
            acc = acc + ref[k].astype(F32)
        return acc

    def two_rows(ref, block, first):
        rows = ref[pl.ds(pl.multiple_of(block * 8, 8), 8), :]
        at = lax.broadcasted_iota(jnp.int32, rows.shape, 0)
        picked = [
            jnp.sum(jnp.where(at == first + k, rows, 0.0), axis=0, keepdims=True) for k in range(2)
        ]
        return jnp.concatenate(picked, axis=0)

    cp_down.wait()
    cp_learn.wait()
    low_in[...] = dot(down[...].astype(BF), learn[...], 1, 1)
    own = pl.ds(pl.multiple_of(c * 32, 32), 32)
    theirs = pl.ds(pl.multiple_of(oc * 32, 32), 32)
    u_send[...] = low_in[theirs, :].astype(BF)
    cp_up.wait()
    cp_cot.wait()
    lowout[...] = dot(cot[...], upt[...].astype(BF), 1, 1).astype(BF)
    term = dot(lowout[...], learn[...], 0, 0).astype(BF)
    for k in range(NO):
        i, j = k // 2, k % 2
        td_send[k] = term[32 * i:32 * i + 32, 256 * j:256 * j + 256]

    pl.semaphore_wait(barrier, 2 * (NA - 1) + (NW - 1) + 1 + 2 * zb)

    remote(u_send, u_prec, U_PAIR, pair).start()

    def to_owner(o, _):
        place, dev = owner_of(o)

        @pl.when(place != a)
        def _():
            remote(td_send.at[o], d_a.at[a], D_A, dev).start()
        return 0

    lax.fori_loop(0, NO, to_owner, 0)

    for k in range(NB - 1):
        @pl.when(k < zb)
        def _():
            for at in (za, GZ - 1 - za):
                pl.semaphore_signal(
                    entered, inc=1, device_id=column(k, at), device_id_type=pl.DeviceIdType.MESH
                )

    @pl.when(owner)
    def _():
        d_a[a] = td_send[mine]

    cp_dec.wait()
    cp_base.wait()

    def other_half(r, _):
        to = pl.ds(pl.multiple_of(r * 256, 256), 256)
        cols = pl.ds(pl.multiple_of(oc * 512 + r * 256, 256), 256)
        m_send[:, to] = dot(dec[...], base[:, cols], 1, 0).astype(BF)
        return 0

    def own_half(r, _):
        to = pl.ds(pl.multiple_of(r * 256, 256), 256)
        cols = pl.ds(pl.multiple_of(c * 512 + r * 256, 256), 256)
        m_keep[:, to] = dot(dec[...], base[:, cols], 1, 0)
        return 0

    lax.fori_loop(0, 2, other_half, 0)
    remote(m_send, m_prec, M_PAIR, pair).start()

    arrived(u_prec, U_PAIR)
    pair_in = (low_in[own, :] + u_prec[...].astype(F32)).astype(BF)
    term_up = dot(pair_in, cot[...], 1, 0).astype(BF)
    for i in range(2):
        for j in range(NC):
            u_sum[i * NC + j] = term_up[16 * i:16 * i + 16, 128 * j:128 * j + 128]
    u_rs[w] = u_sum[w]
    each(NW, wide, U_RS, lambda o: u_sum.at[o], u_rs.at[w])

    remote(dec, dec_p, DEC_PAIR, pair).start()
    remote(down.at[theirs], down_p, DOWN_PAIR, pair).start()

    lax.fori_loop(0, 2, own_half, 0)
    arrived(m_prec, M_PAIR)

    def add_half(r, _):
        rows = pl.ds(pl.multiple_of(r * 64, 64), 64)
        m_sum[r] = (m_keep[rows, :] + m_prec[rows, :].astype(F32)).astype(BF)
        return 0

    lax.fori_loop(0, NC, add_half, 0)
    m_rs[q] = m_sum[q]

    each(NC, chip, M_RS, lambda o: m_sum.at[o], m_rs.at[q])

    @pl.when(owner)
    def _():
        arrived(d_a.at[pl.ds(0, NA - 1)], D_A)
        d_b[zb] = total_of(d_a).astype(BF)
        far_send(D_B, far_down, d_b, "lower")

    arrived(u_rs.at[pl.ds(0, NW - 1)], U_RS)
    u_a[za] = total_of(u_rs).astype(BF)
    for k in range(1, GZ):
        remote(u_a.at[za], u_a.at[za], U_A, above(k)).start()

    arrived(u_a.at[pl.ds(0, GZ - 1)], U_A)
    u_b[zb] = total_of(u_a).astype(BF)
    far_send(U_B, far_up, u_b, "lower")

    my_rows = pl.ds(pl.multiple_of(q * 64, 64), 64)
    arrived(m_rs.at[pl.ds(0, NC - 1)], M_RS)
    m_fin[c, my_rows, :] = total_of(m_rs).astype(BF)
    each(NC, chip, M_AG, lambda o: m_fin.at[c, my_rows], m_fin.at[c, my_rows])

    @pl.when(zb < NB - 1)
    def _():
        pl.semaphore_wait(entered, 2 * (NB - 1 - zb))

    @pl.when(owner)
    def _():
        far_send(D_B, far_down, d_b, "higher")

    far_send(U_B, far_up, u_b, "higher")

    def acts(r, _):
        cols = pl.ds(pl.multiple_of(r * 256, 256), 256)
        ga[:, cols] = (
            dot(cot[...], base[cols, :], 1, 1) + dot(lowout[...], down[:, cols].astype(BF), 1, 0)
        ).astype(BF)
        return 0

    lax.fori_loop(0, 2, acts, 0)

    @pl.when(owner)
    def _():
        far_wait(D_B, d_b)
        d_o[...] = total_of(d_b).astype(BF)
        slot = c * 2 + mine % 2

        def to_core(k, _):
            remote(d_o, d_c.at[slot], D_C, near_core(k, x)).start()
            return 0

        lax.fori_loop(1, NA, to_core, 0)

        @pl.when(x == c)
        def _():
            d_c[slot] = d_o[...]

        @pl.when(x != c)
        def _():
            remote(d_o, d_c.at[slot], D_C, pair).start()

    arrived(dec_p, DEC_PAIR)
    arrived(down_p, DOWN_PAIR)
    holds = jnp.logical_and(owner, x == c)

    @pl.when(holds)
    def _():
        arrived(d_c.at[pl.ds(0, NO - 1)], D_C)

    @pl.when(jnp.logical_not(holds))
    def _():
        arrived(d_c, D_C)

    for j in range(2):
        cols = pl.ds(256 * j, 256)
        ndown[:, cols] = down[own, cols] - rate_down * (d_c[c * 2 + j].astype(F32) / total)
        ndown_p[:, cols] = down_p[:, cols] - rate_down * (d_c[oc * 2 + j].astype(F32) / total)
    l_all[q] = (
        dot(ndown[...].astype(BF), dec[...], 1, 1) + dot(ndown_p[...].astype(BF), dec_p[...], 1, 1)
    ).astype(BF)
    each(NC, chip, L_ALL, lambda o: l_all.at[q], l_all.at[q])

    @pl.when(x == c)
    def _():
        nd_out[...] = two_rows(ndown, z // 4, 2 * (z % 4))
        nd_send[...] = jnp.concatenate([two_rows(ndown_p, z // 4, 2 * (z % 4))] * 4, axis=0)
        remote(nd_send, nd_prec, ND_PAIR, pair).start()

    far_wait(U_B, u_b)
    u_fin[c, w] = total_of(u_b).astype(BF)
    each(NW, wide, U_AG, lambda o: u_fin.at[c, w], u_fin.at[c, w])

    arrived(m_fin.at[c, pl.ds(0, 448)], M_AG)
    remote(m_fin.at[c], m_fin.at[c], M_PAIR2, pair).start()
    arrived(m_fin.at[oc], M_PAIR2)
    cp_m = load(m_fin, m_h, O_M)

    @pl.when(x != c)
    def _():
        arrived(nd_prec, ND_PAIR)
        nd_out[...] = nd_prec[0:2, :]

    arrived(u_fin.at[c, pl.ds(0, NW - 1)], U_AG)
    remote(u_fin.at[c], u_fin.at[c], U_PAIR2, pair).start()

    arrived(l_all.at[pl.ds(0, NC - 1)], L_ALL)
    l_fin[own, :] = total_of(l_all).astype(BF)
    remote(l_fin.at[own], l_fin.at[own], L_PAIR2, pair).start()

    arrived(u_fin.at[oc], U_PAIR2)
    for i in range(4):
        for j in range(NC):
            rows, cols = pl.ds(16 * i, 16), pl.ds(128 * j, 128)
            grad = u_fin[i // 2, (i % 2) * NC + j].astype(F32) / total
            new = upt[rows, cols] - rate_up * grad
            upt[rows, cols] = new
            nupt16[rows, cols] = new.astype(BF)
    first = d * 32 + t * 2
    nup[...] = upt[:, pl.ds(pl.multiple_of(first // 128 * 128, 128), 128)].T
    nu_out[...] = two_rows(nup, first % 128 // 8, first % 8)

    arrived(l_fin.at[own], L_PAIR2)

    m_part = m_fin.at[c, pl.ds(0, 448)]
    for ref, i in (
        (u_send, U_PAIR), (u_rs.at[pl.ds(0, NW - 1)], U_RS),
        (u_a.at[pl.ds(0, GZ - 1)], U_A), (u_b.at[pl.ds(0, NB - 1)], U_B),
        (u_fin.at[c, pl.ds(0, NW - 1)], U_AG), (u_fin.at[c], U_PAIR2), (m_send, M_PAIR),
        (m_rs.at[pl.ds(0, NC - 1)], M_RS), (m_part, M_AG), (m_fin.at[c], M_PAIR2),
        (dec, DEC_PAIR), (down.at[theirs], DOWN_PAIR), (l_all.at[pl.ds(0, NC - 1)], L_ALL), (l_fin.at[own], L_PAIR2),
    ):
        sent(ref, i)

    @pl.when(owner)
    def _():
        sent(td_send.at[pl.ds(0, NO - 1)], D_A)
        sent(d_b.at[pl.ds(0, NB - 1)], D_B)

        @pl.when(x == c)
        def _():
            sent(d_a.at[pl.ds(0, NA - 1)], D_C)

        @pl.when(x != c)
        def _():
            sent(d_a, D_C)

    @pl.when(x == c)
    def _():
        sent(nd_send, ND_PAIR)

    @pl.when(jnp.logical_not(owner))
    def _():
        sent(td_send, D_A)

    cp_m.wait()


def finish_kernel(m_ref, ld_ref, nut_ref, ga_ref, nd_ref, nu_ref, dec_h, ga_h, nd_h, nu_h, dec_v, sem):
    small = [
        pltpu.make_async_copy(ref, out, sem.at[4 + i])
        for i, (ref, out) in enumerate(((ga_ref, ga_h), (nd_ref, nd_h), (nu_ref, nu_h)))
    ]
    for cp in small:
        cp.start()
    parts = []
    for r in range(4):
        rows = slice(128 * r, 128 * r + 128)
        corr = dot(ld_ref[:, rows], nut_ref[...], 0, 0)
        for h in range(2):
            cols = slice(512 * h, 512 * h + 512)
            dec_v[rows, cols] = (m_ref[h, rows, :].astype(F32) + corr[:, cols]).astype(BF)
        cp = pltpu.make_async_copy(dec_v.at[rows], dec_h.at[rows], sem.at[r])
        cp.start()
        parts.append(cp)
    for cp in parts + small:
        cp.wait()


def body(learn_acts, cotangent, base_weight, down_factor, up_factor, decode_acts):
    any_ = pl.BlockSpec(memory_space=pl.ANY)
    hbm = pl.BlockSpec(memory_space=pltpu.HBM)
    vmem = pl.BlockSpec(memory_space=pltpu.VMEM)
    V = pltpu.VMEM
    sds = jax.ShapeDtypeStruct
    ga, nd, nu, nut, ld, m = pl.pallas_call(
        comm_kernel,
        out_shape=(
            sds((512, 512), BF), sds((2, 512), F32), sds((2, 64), F32),
            sds((64, 1024), BF), sds((64, 512), BF), sds((2, 512, 512), BF),
        ),
        in_specs=[hbm] * 6,
        out_specs=(vmem,) * 5 + (any_,),
        scratch_shapes=[
            V((512, 512), BF), V((512, 1024), BF), V((512, 1024), BF), V((64, 512), F32),
            V((512, 512), BF), V((512, 512), BF), V((32, 512), F32),
            V((512, 64), BF), V((64, 512), F32), V((NO, 32, 256), BF), V((NA, 32, 256), BF),
            V((NB, 32, 256), BF), V((32, 256), BF), V((NO, 32, 256), BF), V((32, 512), F32),
            V((32, 512), F32), V((8, 512), F32), V((8, 512), F32),
            V((32, 512), BF), V((32, 512), BF), V((NW, 16, 128), BF), V((NW, 16, 128), BF),
            V((GZ, 16, 128), BF), V((NB, 16, 128), BF), V((2, NW, 16, 128), BF),
            V((64, 1024), F32), V((128, 64), F32),
            V((512, 512), BF), V((512, 512), F32), V((512, 512), BF), V((NC, 64, 512), BF),
            V((NC, 64, 512), BF), V((2, 512, 512), BF), V((NC, 32, 512), BF),
            pltpu.SemaphoreType.DMA((18,)), pltpu.SemaphoreType.DMA((18,)),
            pltpu.SemaphoreType.DMA((16, NB)),
            pltpu.SemaphoreType.DMA((7,)), pltpu.SemaphoreType.REGULAR,
        ],
        compiler_params=pltpu.CompilerParams(
            collective_id=0, has_side_effects=True, vmem_limit_bytes=48 * 1024 * 1024
        ),
        name="adapter_step",
    )(*(
        pltpu.with_memory_space_constraint(arg, pltpu.HBM)
        for arg in (
            learn_acts, cotangent, base_weight, down_factor, up_factor.T, decode_acts
        )
    ))
    decoded, ga, nd, nu = pl.pallas_call(
        finish_kernel,
        out_shape=(
            sds((512, 1024), BF), sds((512, 512), BF), sds((2, 512), F32), sds((2, 64), F32),
        ),
        in_specs=[vmem] * 6,
        out_specs=(hbm,) * 4,
        scratch_shapes=[V((512, 1024), BF), pltpu.SemaphoreType.DMA((7,))],
        compiler_params=pltpu.CompilerParams(vmem_limit_bytes=16 * 1024 * 1024),
        name="finish",
    )(m, ld, nut, ga, nd, nu)
    return (ga, nd, nu, decoded)


def solution(mesh):
    in_specs = (
        P("dp", "tensor"),
        P("dp", None),
        P("tensor", None),
        P(None, "tensor"),
        P(),
        P("dp", "tensor"),
    )
    out_specs = (P("dp", "tensor"), P("dp", "tensor"), P(("dp", "tensor"), None), P("dp", None))
    return jax.shard_map(body, mesh=mesh, in_specs=in_specs, out_specs=out_specs, check_vma=False)
```

```python
import jax
import jax.numpy as jnp
from jax import lax
from jax.experimental import pallas as pl
from jax.experimental.pallas import tpu as pltpu
from jax.sharding import PartitionSpec as P

rate_down = 0.2
rate_up = 3.0

NZ = 16
GZ = 4
NA = 8
NB = 4
NO = 4
NC = 8
NW = 16

BF = jnp.bfloat16
F32 = jnp.float32

(D_A, D_B, D_C, U_PAIR, U_RS, U_A, U_B, U_AG, U_PAIR2,
 M_PAIR, M_RS, M_AG, M_PAIR2, DEC_PAIR, L_ALL, L_PAIR2, DOWN_PAIR, ND_PAIR,
 D_A2, D_B2, D_C2) = range(21)
DA, DB, DC = (D_A, D_A2), (D_B, D_B2), (D_C, D_C2)
(I_COT, I_UP, I_LEARN, I_DOWN, I_DEC, I_BASE, O_M) = range(7)


def dot(a, b, ca, cb):
    return lax.dot_general(a, b, (((ca,), (cb,)), ((), ())), preferred_element_type=F32)


def div(a, b):
    return lax.div(a, jnp.int32(b))


def rem(a, b):
    return lax.rem(a, jnp.int32(b))


def comm_kernel(
    learn_h, cot_h, base_h, down_h, up_h, dec_h,
    ga, nd_out, nu_out, nupt16, l_fin, m_h,
    learn, cot, base, down, dec, dec_p, down_p,
    lowout, low_in, td_send, d_a, d_b, d_o, d_c, ndown, ndown_p, nd_send, nd_prec,
    u_send, u_prec, u_sum, u_rs, u_a, u_b, u_fin, upt, nup,
    m_send, m_keep, m_prec, m_sum, m_rs, m_fin, l_all,
    ssem, rsem, rfar, lsem, entered,
):
    d = lax.axis_index("dp")
    t = lax.axis_index("tensor")
    x = div(d, NZ)
    z = rem(d, NZ)
    zb = div(z, GZ)
    za = rem(z, GZ)
    a = x * GZ + za
    q = div(t, 2)
    c = rem(t, 2)
    oc = 1 - c
    w = x * NC + q
    total = 16384.0

    def load(src, dst, i):
        cp = pltpu.make_async_copy(src, dst, lsem.at[i])
        cp.start()
        return cp

    cp_down = load(down_h, down, I_DOWN)
    cp_learn = load(learn_h, learn, I_LEARN)
    cp_up = load(up_h, upt, I_UP)
    cp_cot = load(cot_h, cot, I_COT)
    cp_dec = load(dec_h, dec, I_DEC)
    cp_base = load(base_h, base, I_BASE)

    def first_owner(group):
        return jnp.where(group == 0, 0, 1)

    part = za - first_owner(zb)
    owner = jnp.logical_or(part == 0, part == 1)
    mine = x * 2 + part

    def near(k):
        other = rem(a + k, NA)
        return other, {"dp": div(other, GZ) * NZ + zb * GZ + rem(other, GZ), "tensor": t}

    def near_core(k, core):
        return {"dp": near(k)[1]["dp"], "tensor": q * 2 + core}

    def owner_of(o):
        at = first_owner(zb) + o % 2
        return (o // 2) * GZ + at, {"dp": (o // 2) * NZ + zb * GZ + at, "tensor": t}

    def column(group, at):
        return {"dp": x * NZ + group * GZ + at, "tensor": t}

    def far_down(k):
        return column(k, first_owner(k) + part)

    def far_up(k):
        opposite = jnp.logical_or(zb == k + 2, zb == k - 2)
        return column(k, jnp.where(opposite, GZ - 1 - za, za))

    def wide(k):
        other = rem(w + k, NW)
        return other, {"dp": div(other, NC) * NZ + z, "tensor": rem(other, NC) * 2 + c}

    def above(k):
        return {"dp": x * NZ + zb * GZ + rem(za + k, GZ), "tensor": t}

    def chip(k):
        other = rem(q + k, NC)
        return other, {"dp": d, "tensor": other * 2 + c}

    pair = {"dp": d, "tensor": q * 2 + oc}

    barrier = pltpu.get_barrier_semaphore()

    def greet(dev):
        pl.semaphore_signal(barrier, inc=1, device_id=dev, device_id_type=pl.DeviceIdType.MESH)

    def hello_near(k, _):
        for core in range(2):
            greet(near_core(k, core))
        return 0

    def hello_wide(k, _):
        greet(wide(k)[1])
        return 0

    for k in range(1, NA):
        hello_near(k, 0)
    for k in range(1, NW):
        hello_wide(k, 0)
    greet(pair)
    for k in range(1, NB):
        @pl.when(zb < k)
        def _():
            greet(far_up(k))

        @pl.when(jnp.logical_and(zb < k, owner))
        def _():
            greet(far_down(k))

    def remote(src, dst, i, dev):
        return pltpu.make_async_remote_copy(
            src_ref=src, dst_ref=dst, send_sem=ssem.at[i], recv_sem=rsem.at[i],
            device_id=dev, device_id_type=pl.DeviceIdType.MESH,
        )

    def arrived(ref, i):
        remote(ref, ref, i, pair).wait_recv()

    def sent(ref, i):
        remote(ref, ref, i, pair).wait_send()

    def each(n, place, i, src, dst):
        def step(k, _):
            other, dev = place(k)
            remote(src(other), dst, i, dev).start()
            return 0
        for k in range(1, n):
            step(k, 0)

    def send_far(i, dev, buf, k):
        pltpu.make_async_remote_copy(
            src_ref=buf.at[zb], dst_ref=buf.at[zb], send_sem=ssem.at[i],
            recv_sem=rfar.at[i, zb], device_id=dev(k), device_id_type=pl.DeviceIdType.MESH,
        ).start()

    def far_arrived(i, buf, k):
        pltpu.make_async_remote_copy(
            src_ref=buf.at[k], dst_ref=buf.at[k], send_sem=ssem.at[i],
            recv_sem=rfar.at[i, k], device_id=pair, device_id_type=pl.DeviceIdType.MESH,
        ).wait_recv()

    def far_send(i, dev, buf, wanted):
        for step in (1, 3, 2):
            k = rem(zb + step, NB)

            @pl.when(k > zb if wanted == "higher" else k < zb)
            def _():
                send_far(i, dev, buf, k)

    def far_wait(i, buf):
        for step in range(1, NB):
            far_arrived(i, buf, rem(zb + step, NB))

    def total_of(ref):
        acc = ref[0].astype(F32)
        for k in range(1, ref.shape[0]):
            acc = acc + ref[k].astype(F32)
        return acc

    def two_rows(ref, block, first):
        rows = ref[pl.ds(pl.multiple_of(block * 8, 8), 8), :]
        at = lax.broadcasted_iota(jnp.int32, rows.shape, 0)
        picked = [
            jnp.sum(jnp.where(at == first + k, rows, 0.0), axis=0, keepdims=True) for k in range(2)
        ]
        return jnp.concatenate(picked, axis=0)

    cp_down.wait()
    cp_learn.wait()
    low_in[...] = dot(down[...].astype(BF), learn[...], 1, 1)
    own = pl.ds(pl.multiple_of(c * 32, 32), 32)
    theirs = pl.ds(pl.multiple_of(oc * 32, 32), 32)
    u_send[...] = low_in[theirs, :].astype(BF)
    cp_up.wait()
    cp_cot.wait()
    lowout[...] = dot(cot[...], upt[...].astype(BF), 1, 1).astype(BF)
    term = dot(lowout[...], learn[...], 0, 0).astype(BF)
    for k in range(NO):
        i, j = k // 2, k % 2
        for h in range(2):
            td_send[h, k] = term[32 * i:32 * i + 32, 256 * j + 128 * h:256 * j + 128 * h + 128]

    far_greets = 1 + owner.astype(jnp.int32)
    pl.semaphore_wait(barrier, 2 * (NA - 1) + (NW - 1) + 1 + far_greets * zb)

    remote(u_send, u_prec, U_PAIR, pair).start()

    for h in range(2):
        for o in range(NO):
            place, dev = owner_of(o)

            @pl.when(place != a)
            def _():
                remote(td_send.at[h, o], d_a.at[h, a], DA[h], dev).start()

    for k in range(NB - 1):
        @pl.when(k < zb)
        def _():
            pl.semaphore_signal(
                entered, inc=1, device_id=far_up(k), device_id_type=pl.DeviceIdType.MESH
            )

        @pl.when(jnp.logical_and(k < zb, owner))
        def _():
            pl.semaphore_signal(
                entered, inc=1, device_id=far_down(k), device_id_type=pl.DeviceIdType.MESH
            )

    @pl.when(owner)
    def _():
        for h in range(2):
            d_a[h, a] = td_send[h, mine]

    cp_dec.wait()
    cp_base.wait()

    def other_half(r, _):
        to = pl.ds(pl.multiple_of(r * 256, 256), 256)
        cols = pl.ds(pl.multiple_of(oc * 512 + r * 256, 256), 256)
        m_send[:, to] = dot(dec[...], base[:, cols], 1, 0).astype(BF)
        return 0

    def own_half(r, _):
        to = pl.ds(pl.multiple_of(r * 256, 256), 256)
        cols = pl.ds(pl.multiple_of(c * 512 + r * 256, 256), 256)
        m_keep[:, to] = dot(dec[...], base[:, cols], 1, 0)
        return 0

    lax.fori_loop(0, 2, other_half, 0)
    remote(m_send, m_prec, M_PAIR, pair).start()

    arrived(u_prec, U_PAIR)
    pair_in = (low_in[own, :] + u_prec[...].astype(F32)).astype(BF)
    term_up = dot(pair_in, cot[...], 1, 0).astype(BF)
    for i in range(2):
        for j in range(NC):
            u_sum[i * NC + j] = term_up[16 * i:16 * i + 16, 128 * j:128 * j + 128]
    u_rs[w] = u_sum[w]
    each(NW, wide, U_RS, lambda o: u_sum.at[o], u_rs.at[w])

    remote(dec, dec_p, DEC_PAIR, pair).start()
    remote(down.at[theirs], down_p, DOWN_PAIR, pair).start()

    lax.fori_loop(0, 2, own_half, 0)
    arrived(m_prec, M_PAIR)

    def add_half(r, _):
        rows = pl.ds(pl.multiple_of(r * 64, 64), 64)
        m_sum[r] = (m_keep[rows, :] + m_prec[rows, :].astype(F32)).astype(BF)
        return 0

    lax.fori_loop(0, NC, add_half, 0)
    m_rs[q] = m_sum[q]

    each(NC, chip, M_RS, lambda o: m_sum.at[o], m_rs.at[q])

    @pl.when(owner)
    def _():
        for h in range(2):
            arrived(d_a.at[h, pl.ds(0, NA - 1)], DA[h])
            d_b[h, zb] = total_of(d_a.at[h]).astype(BF)
            far_send(DB[h], far_down, d_b.at[h], "lower")

    arrived(u_rs.at[pl.ds(0, NW - 1)], U_RS)
    u_a[za] = total_of(u_rs).astype(BF)
    for k in range(1, GZ):
        remote(u_a.at[za], u_a.at[za], U_A, above(k)).start()

    arrived(u_a.at[pl.ds(0, GZ - 1)], U_A)
    u_b[zb] = total_of(u_a).astype(BF)
    far_send(U_B, far_up, u_b, "lower")

    my_rows = pl.ds(pl.multiple_of(q * 64, 64), 64)
    arrived(m_rs.at[pl.ds(0, NC - 1)], M_RS)
    m_fin[c, my_rows, :] = total_of(m_rs).astype(BF)
    each(NC, chip, M_AG, lambda o: m_fin.at[c, my_rows], m_fin.at[c, my_rows])

    @pl.when(zb < NB - 1)
    def _():
        pl.semaphore_wait(entered, far_greets * (NB - 1 - zb))

    @pl.when(owner)
    def _():
        for h in range(2):
            far_send(DB[h], far_down, d_b.at[h], "higher")

    far_send(U_B, far_up, u_b, "higher")

    def acts(r, _):
        cols = pl.ds(pl.multiple_of(r * 256, 256), 256)
        ga[:, cols] = (
            dot(cot[...], base[cols, :], 1, 1) + dot(lowout[...], down[:, cols].astype(BF), 1, 0)
        ).astype(BF)
        return 0

    lax.fori_loop(0, 2, acts, 0)

    @pl.when(owner)
    def _():
        slot = c * 2 + part
        for h in range(2):
            far_wait(DB[h], d_b.at[h])
            d_o[h] = total_of(d_b.at[h]).astype(BF)
            for k in range(1, NA):
                remote(d_o.at[h], d_c.at[h, slot], DC[h], near_core(k, x)).start()

            @pl.when(x == c)
            def _():
                d_c[h, slot] = d_o[h]

            @pl.when(x != c)
            def _():
                remote(d_o.at[h], d_c.at[h, slot], DC[h], pair).start()

    arrived(dec_p, DEC_PAIR)
    arrived(down_p, DOWN_PAIR)
    holds = jnp.logical_and(owner, x == c)

    for h in range(2):
        @pl.when(holds)
        def _():
            arrived(d_c.at[h, pl.ds(0, NO - 1)], DC[h])

        @pl.when(jnp.logical_not(holds))
        def _():
            arrived(d_c.at[h], DC[h])

        for j in range(2):
            cols = pl.ds(256 * j + 128 * h, 128)
            ndown[:, cols] = down[own, cols] - rate_down * (d_c[h, c * 2 + j].astype(F32) / total)
            ndown_p[:, cols] = down_p[:, cols] - rate_down * (d_c[h, oc * 2 + j].astype(F32) / total)
    l_all[q] = (
        dot(ndown[...].astype(BF), dec[...], 1, 1) + dot(ndown_p[...].astype(BF), dec_p[...], 1, 1)
    ).astype(BF)
    each(NC, chip, L_ALL, lambda o: l_all.at[q], l_all.at[q])

    @pl.when(x == c)
    def _():
        nd_out[...] = two_rows(ndown, div(z, 4), 2 * rem(z, 4))
        nd_send[...] = jnp.concatenate([two_rows(ndown_p, div(z, 4), 2 * rem(z, 4))] * 4, axis=0)
        remote(nd_send, nd_prec, ND_PAIR, pair).start()

    far_wait(U_B, u_b)
    u_fin[c, w] = total_of(u_b).astype(BF)
    each(NW, wide, U_AG, lambda o: u_fin.at[c, w], u_fin.at[c, w])

    arrived(m_fin.at[c, pl.ds(0, 448)], M_AG)
    remote(m_fin.at[c], m_fin.at[c], M_PAIR2, pair).start()
    arrived(m_fin.at[oc], M_PAIR2)
    cp_m = load(m_fin, m_h, O_M)

    @pl.when(x != c)
    def _():
        arrived(nd_prec, ND_PAIR)
        nd_out[...] = nd_prec[0:2, :]

    arrived(u_fin.at[c, pl.ds(0, NW - 1)], U_AG)
    remote(u_fin.at[c], u_fin.at[c], U_PAIR2, pair).start()

    arrived(l_all.at[pl.ds(0, NC - 1)], L_ALL)
    l_fin[own, :] = total_of(l_all).astype(BF)
    remote(l_fin.at[own], l_fin.at[own], L_PAIR2, pair).start()

    arrived(u_fin.at[oc], U_PAIR2)
    for i in range(4):
        for j in range(NC):
            rows, cols = pl.ds(16 * i, 16), pl.ds(128 * j, 128)
            grad = u_fin[i // 2, (i % 2) * NC + j].astype(F32) / total
            new = upt[rows, cols] - rate_up * grad
            upt[rows, cols] = new
            nupt16[rows, cols] = new.astype(BF)
    first = d * 32 + t * 2
    nup[...] = upt[:, pl.ds(pl.multiple_of(div(first, 128) * 128, 128), 128)].T
    nu_out[...] = two_rows(nup, div(rem(first, 128), 8), rem(first, 8))

    arrived(l_fin.at[own], L_PAIR2)

    m_part = m_fin.at[c, pl.ds(0, 448)]
    for ref, i in (
        (u_send, U_PAIR), (u_rs.at[pl.ds(0, NW - 1)], U_RS),
        (u_a.at[pl.ds(0, GZ - 1)], U_A), (u_b.at[pl.ds(0, NB - 1)], U_B),
        (u_fin.at[c, pl.ds(0, NW - 1)], U_AG), (u_fin.at[c], U_PAIR2), (m_send, M_PAIR),
        (m_rs.at[pl.ds(0, NC - 1)], M_RS), (m_part, M_AG), (m_fin.at[c], M_PAIR2),
        (dec, DEC_PAIR), (down.at[theirs], DOWN_PAIR), (l_all.at[pl.ds(0, NC - 1)], L_ALL), (l_fin.at[own], L_PAIR2),
    ):
        sent(ref, i)

    for h in range(2):
        @pl.when(owner)
        def _():
            sent(td_send.at[h, pl.ds(0, NO - 1)], DA[h])
            sent(d_b.at[h, pl.ds(0, NB - 1)], DB[h])

            @pl.when(x == c)
            def _():
                sent(d_a.at[h, pl.ds(0, NA - 1)], DC[h])

            @pl.when(x != c)
            def _():
                sent(d_a.at[h], DC[h])

        @pl.when(jnp.logical_not(owner))
        def _():
            sent(td_send.at[h], DA[h])

    @pl.when(x == c)
    def _():
        sent(nd_send, ND_PAIR)


    cp_m.wait()


def finish_kernel(m_ref, ld_ref, nut_ref, ga_ref, nd_ref, nu_ref, dec_h, ga_h, nd_h, nu_h, dec_v, sem):
    small = [
        pltpu.make_async_copy(ref, out, sem.at[4 + i])
        for i, (ref, out) in enumerate(((ga_ref, ga_h), (nd_ref, nd_h), (nu_ref, nu_h)))
    ]
    for cp in small:
        cp.start()
    parts = []
    for r in range(4):
        rows = slice(128 * r, 128 * r + 128)
        corr = dot(ld_ref[:, rows], nut_ref[...], 0, 0)
        for h in range(2):
            cols = slice(512 * h, 512 * h + 512)
            dec_v[rows, cols] = (m_ref[h, rows, :].astype(F32) + corr[:, cols]).astype(BF)
        cp = pltpu.make_async_copy(dec_v.at[rows], dec_h.at[rows], sem.at[r])
        cp.start()
        parts.append(cp)
    for cp in parts + small:
        cp.wait()


def body(learn_acts, cotangent, base_weight, down_factor, up_factor, decode_acts):
    any_ = pl.BlockSpec(memory_space=pl.ANY)
    hbm = pl.BlockSpec(memory_space=pltpu.HBM)
    vmem = pl.BlockSpec(memory_space=pltpu.VMEM)
    V = pltpu.VMEM
    sds = jax.ShapeDtypeStruct
    ga, nd, nu, nut, ld, m = pl.pallas_call(
        comm_kernel,
        out_shape=(
            sds((512, 512), BF), sds((2, 512), F32), sds((2, 64), F32),
            sds((64, 1024), BF), sds((64, 512), BF), sds((2, 512, 512), BF),
        ),
        in_specs=[hbm] * 6,
        out_specs=(vmem,) * 5 + (any_,),
        scratch_shapes=[
            V((512, 512), BF), V((512, 1024), BF), V((512, 1024), BF), V((64, 512), F32),
            V((512, 512), BF), V((512, 512), BF), V((32, 512), F32),
            V((512, 64), BF), V((64, 512), F32), V((2, NO, 32, 128), BF), V((2, NA, 32, 128), BF),
            V((2, NB, 32, 128), BF), V((2, 32, 128), BF), V((2, NO, 32, 128), BF), V((32, 512), F32),
            V((32, 512), F32), V((8, 512), F32), V((8, 512), F32),
            V((32, 512), BF), V((32, 512), BF), V((NW, 16, 128), BF), V((NW, 16, 128), BF),
            V((GZ, 16, 128), BF), V((NB, 16, 128), BF), V((2, NW, 16, 128), BF),
            V((64, 1024), F32), V((128, 64), F32),
            V((512, 512), BF), V((512, 512), F32), V((512, 512), BF), V((NC, 64, 512), BF),
            V((NC, 64, 512), BF), V((2, 512, 512), BF), V((NC, 32, 512), BF),
            pltpu.SemaphoreType.DMA((21,)), pltpu.SemaphoreType.DMA((21,)),
            pltpu.SemaphoreType.DMA((21, NB)),
            pltpu.SemaphoreType.DMA((7,)), pltpu.SemaphoreType.REGULAR,
        ],
        compiler_params=pltpu.CompilerParams(
            collective_id=0, has_side_effects=True, vmem_limit_bytes=48 * 1024 * 1024
        ),
        name="adapter_step",
    )(*(
        pltpu.with_memory_space_constraint(arg, pltpu.HBM)
        for arg in (
            learn_acts, cotangent, base_weight, down_factor, up_factor.T, decode_acts
        )
    ))
    decoded, ga, nd, nu = pl.pallas_call(
        finish_kernel,
        out_shape=(
            sds((512, 1024), BF), sds((512, 512), BF), sds((2, 512), F32), sds((2, 64), F32),
        ),
        in_specs=[vmem] * 6,
        out_specs=(hbm,) * 4,
        scratch_shapes=[V((512, 1024), BF), pltpu.SemaphoreType.DMA((7,))],
        compiler_params=pltpu.CompilerParams(vmem_limit_bytes=16 * 1024 * 1024),
        name="finish",
    )(m, ld, nut, ga, nd, nu)
    return (ga, nd, nu, decoded)


def solution(mesh):
    in_specs = (
        P("dp", "tensor"),
        P("dp", None),
        P("tensor", None),
        P(None, "tensor"),
        P(),
        P("dp", "tensor"),
    )
    out_specs = (P("dp", "tensor"), P("dp", "tensor"), P(("dp", "tensor"), None), P("dp", None))
    return jax.shard_map(body, mesh=mesh, in_specs=in_specs, out_specs=out_specs, check_vma=False)
```

```python
import jax
import jax.numpy as jnp
from jax import lax
from jax.experimental import pallas as pl
from jax.experimental.pallas import tpu as pltpu
from jax.sharding import PartitionSpec as P

rate_down = 0.2
rate_up = 3.0

NZ = 16
GZ = 4
NA = 8
NB = 4
NO = 4
NC = 8
NW = 16

FAR_NEAR = (2, 6, 3, 5, 1, 7, 4)
FAR_CHIP = (3, 5, 1, 7, 4, 2, 6)
FAR_WIDE = (3, 13, 5, 11, 4, 12, 1, 15, 6, 10, 7, 9, 2, 14, 8)

BF = jnp.bfloat16
F32 = jnp.float32

(D_A, D_B, D_C, U_PAIR, U_RS, U_A, U_B, U_AG, U_PAIR2,
 M_PAIR, M_RS, M_AG, M_PAIR2, DEC_PAIR, L_Y0, L_PAIR2, DOWN_PAIR, ND_PAIR,
 D_A2, D_B2, D_C2, L_X0, L_X1, L_Y1) = range(24)
DA, DB, DC = (D_A, D_A2), (D_B, D_B2), (D_C, D_C2)
(I_COT, I_UP, I_LEARN, I_DOWN, I_DEC, I_BASE, O_M) = range(7)


def dot(a, b, ca, cb):
    return lax.dot_general(a, b, (((ca,), (cb,)), ((), ())), preferred_element_type=F32)


def div(a, b):
    return lax.div(a, jnp.int32(b))


def rem(a, b):
    return lax.rem(a, jnp.int32(b))


def comm_kernel(
    learn_h, cot_h, base_h, down_h, up_h, dec_h,
    ga, nd_out, nu_out, nupt16, l_fin, m_h,
    learn, cot, base, down, dec, dec_p, down_p,
    lowout, low_in, td_send, d_a, d_b, d_o, d_c, ndown, ndown_p, nd_send, nd_prec,
    u_send, u_prec, u_sum, u_rs, u_a, u_b, u_fin, upt, nup,
    m_send, m_keep, m_prec, m_sum, m_rs, m_fin, l_y0, l_x0, l_x1, l_y1,
    ssem, rsem, rfar, lsem, entered,
):
    d = lax.axis_index("dp")
    t = lax.axis_index("tensor")
    x = div(d, NZ)
    z = rem(d, NZ)
    zb = div(z, GZ)
    za = rem(z, GZ)
    a = x * GZ + za
    q = div(t, 2)
    c = rem(t, 2)
    oc = 1 - c
    yy = div(q, 2)
    xh = rem(q, 2)
    w = x * NC + q
    total = 16384.0

    def load(src, dst, i):
        cp = pltpu.make_async_copy(src, dst, lsem.at[i])
        cp.start()
        return cp

    cp_down = load(down_h, down, I_DOWN)
    cp_learn = load(learn_h, learn, I_LEARN)
    cp_up = load(up_h, upt, I_UP)
    cp_cot = load(cot_h, cot, I_COT)
    cp_dec = load(dec_h, dec, I_DEC)
    cp_base = load(base_h, base, I_BASE)

    def first_owner(group):
        return jnp.where(group == 0, 0, 1)

    part = za - first_owner(zb)
    owner = jnp.logical_or(part == 0, part == 1)
    mine = x * 2 + part

    def near(k):
        other = rem(a + k, NA)
        return other, {"dp": div(other, GZ) * NZ + zb * GZ + rem(other, GZ), "tensor": t}

    def near_core(k, core):
        return {"dp": near(k)[1]["dp"], "tensor": q * 2 + core}

    def owner_of(o):
        at = first_owner(zb) + o % 2
        return (o // 2) * GZ + at, {"dp": (o // 2) * NZ + zb * GZ + at, "tensor": t}

    def column(group, at):
        return {"dp": x * NZ + group * GZ + at, "tensor": t}

    def far_down(k):
        return column(k, first_owner(k) + part)

    def far_up(k):
        opposite = jnp.logical_or(zb == k + 2, zb == k - 2)
        return column(k, jnp.where(opposite, GZ - 1 - za, za))

    def wide(k):
        other = rem(w + k, NW)
        return other, {"dp": div(other, NC) * NZ + z, "tensor": rem(other, NC) * 2 + c}

    def above(k):
        return {"dp": x * NZ + zb * GZ + rem(za + k, GZ), "tensor": t}

    def along_y(k):
        return {"dp": d, "tensor": rem(yy + k, 4) * 4 + xh * 2 + c}

    along_x = {"dp": d, "tensor": yy * 4 + (1 - xh) * 2 + c}

    def chip(k):
        other = rem(q + k, NC)
        return other, {"dp": d, "tensor": other * 2 + c}

    pair = {"dp": d, "tensor": q * 2 + oc}

    barrier = pltpu.get_barrier_semaphore()

    def greet(dev):
        pl.semaphore_signal(barrier, inc=1, device_id=dev, device_id_type=pl.DeviceIdType.MESH)

    def hello_near(k, _):
        for core in range(2):
            greet(near_core(k, core))
        return 0

    def hello_wide(k, _):
        greet(wide(k)[1])
        return 0

    for k in FAR_NEAR:
        hello_near(k, 0)
    for k in FAR_WIDE:
        hello_wide(k, 0)
    greet(pair)
    for k in range(1, NB):
        @pl.when(zb < k)
        def _():
            greet(far_up(k))

        @pl.when(jnp.logical_and(zb < k, owner))
        def _():
            greet(far_down(k))

    def remote(src, dst, i, dev):
        return pltpu.make_async_remote_copy(
            src_ref=src, dst_ref=dst, send_sem=ssem.at[i], recv_sem=rsem.at[i],
            device_id=dev, device_id_type=pl.DeviceIdType.MESH,
        )

    def arrived(ref, i):
        remote(ref, ref, i, pair).wait_recv()

    def sent(ref, i):
        remote(ref, ref, i, pair).wait_send()

    def each(order, place, i, src, dst):
        def step(k, _):
            other, dev = place(k)
            remote(src(other), dst, i, dev).start()
            return 0
        for k in order:
            step(k, 0)

    def send_far(i, dev, buf, k):
        pltpu.make_async_remote_copy(
            src_ref=buf.at[zb], dst_ref=buf.at[zb], send_sem=ssem.at[i],
            recv_sem=rfar.at[i, zb], device_id=dev(k), device_id_type=pl.DeviceIdType.MESH,
        ).start()

    def far_arrived(i, buf, k):
        pltpu.make_async_remote_copy(
            src_ref=buf.at[k], dst_ref=buf.at[k], send_sem=ssem.at[i],
            recv_sem=rfar.at[i, k], device_id=pair, device_id_type=pl.DeviceIdType.MESH,
        ).wait_recv()

    def far_send(i, dev, buf, wanted):
        for step in (1, 3, 2):
            k = rem(zb + step, NB)

            @pl.when(k > zb if wanted == "higher" else k < zb)
            def _():
                send_far(i, dev, buf, k)

    def far_wait(i, buf):
        for step in range(1, NB):
            far_arrived(i, buf, rem(zb + step, NB))

    def total_of(ref):
        acc = ref[0].astype(F32)
        for k in range(1, ref.shape[0]):
            acc = acc + ref[k].astype(F32)
        return acc

    def two_rows(ref, block, first):
        rows = ref[pl.ds(pl.multiple_of(block * 8, 8), 8), :]
        at = lax.broadcasted_iota(jnp.int32, rows.shape, 0)
        picked = [
            jnp.sum(jnp.where(at == first + k, rows, 0.0), axis=0, keepdims=True) for k in range(2)
        ]
        return jnp.concatenate(picked, axis=0)

    cp_down.wait()
    cp_learn.wait()
    low_in[...] = dot(down[...].astype(BF), learn[...], 1, 1)
    own = pl.ds(pl.multiple_of(c * 32, 32), 32)
    theirs = pl.ds(pl.multiple_of(oc * 32, 32), 32)
    u_send[...] = low_in[theirs, :].astype(BF)
    cp_up.wait()
    cp_cot.wait()
    lowout[...] = dot(cot[...], upt[...].astype(BF), 1, 1).astype(BF)
    term = dot(lowout[...], learn[...], 0, 0).astype(BF)
    for k in range(NO):
        i, j = k // 2, k % 2
        for h in range(2):
            td_send[h, k] = term[32 * i:32 * i + 32, 256 * j + 128 * h:256 * j + 128 * h + 128]

    far_greets = 1 + owner.astype(jnp.int32)
    pl.semaphore_wait(barrier, 2 * (NA - 1) + (NW - 1) + 1 + far_greets * zb)

    remote(u_send, u_prec, U_PAIR, pair).start()

    for h in range(2):
        for o in range(NO):
            place, dev = owner_of(o)

            @pl.when(place != a)
            def _():
                remote(td_send.at[h, o], d_a.at[h, a], DA[h], dev).start()

    for k in range(NB - 1):
        @pl.when(k < zb)
        def _():
            pl.semaphore_signal(
                entered, inc=1, device_id=far_up(k), device_id_type=pl.DeviceIdType.MESH
            )

        @pl.when(jnp.logical_and(k < zb, owner))
        def _():
            pl.semaphore_signal(
                entered, inc=1, device_id=far_down(k), device_id_type=pl.DeviceIdType.MESH
            )

    @pl.when(owner)
    def _():
        for h in range(2):
            d_a[h, a] = td_send[h, mine]

    arrived(u_prec, U_PAIR)
    pair_in = (low_in[own, :] + u_prec[...].astype(F32)).astype(BF)
    term_up = dot(pair_in, cot[...], 1, 0).astype(BF)
    for i in range(2):
        for j in range(NC):
            u_sum[i * NC + j] = term_up[16 * i:16 * i + 16, 128 * j:128 * j + 128]
    u_rs[w] = u_sum[w]
    each(FAR_WIDE, wide, U_RS, lambda o: u_sum.at[o], u_rs.at[w])

    cp_dec.wait()
    cp_base.wait()

    def other_half(r, _):
        to = pl.ds(pl.multiple_of(r * 256, 256), 256)
        cols = pl.ds(pl.multiple_of(oc * 512 + r * 256, 256), 256)
        m_send[:, to] = dot(dec[...], base[:, cols], 1, 0).astype(BF)
        return 0

    def own_half(r, _):
        to = pl.ds(pl.multiple_of(r * 256, 256), 256)
        cols = pl.ds(pl.multiple_of(c * 512 + r * 256, 256), 256)
        m_keep[:, to] = dot(dec[...], base[:, cols], 1, 0)
        return 0

    lax.fori_loop(0, 2, other_half, 0)
    remote(m_send, m_prec, M_PAIR, pair).start()

    remote(dec, dec_p, DEC_PAIR, pair).start()
    remote(down.at[theirs], down_p, DOWN_PAIR, pair).start()

    lax.fori_loop(0, 2, own_half, 0)
    @pl.when(owner)
    def _():
        for h in range(2):
            arrived(d_a.at[h, pl.ds(0, NA - 1)], DA[h])
            d_b[h, zb] = total_of(d_a.at[h]).astype(BF)
            far_send(DB[h], far_down, d_b.at[h], "lower")

    arrived(m_prec, M_PAIR)

    def add_half(r, _):
        rows = pl.ds(pl.multiple_of(r * 64, 64), 64)
        m_sum[r] = (m_keep[rows, :] + m_prec[rows, :].astype(F32)).astype(BF)
        return 0

    lax.fori_loop(0, NC, add_half, 0)
    m_rs[q] = m_sum[q]

    each(FAR_CHIP, chip, M_RS, lambda o: m_sum.at[o], m_rs.at[q])

    arrived(u_rs.at[pl.ds(0, NW - 1)], U_RS)
    u_a[za] = total_of(u_rs).astype(BF)
    for k in range(1, GZ):
        remote(u_a.at[za], u_a.at[za], U_A, above(k)).start()

    arrived(u_a.at[pl.ds(0, GZ - 1)], U_A)
    u_b[zb] = total_of(u_a).astype(BF)
    far_send(U_B, far_up, u_b, "lower")

    my_rows = pl.ds(pl.multiple_of(q * 64, 64), 64)
    arrived(m_rs.at[pl.ds(0, NC - 1)], M_RS)
    m_fin[c, my_rows, :] = total_of(m_rs).astype(BF)
    each(FAR_CHIP, chip, M_AG, lambda o: m_fin.at[c, my_rows], m_fin.at[c, my_rows])

    @pl.when(zb < NB - 1)
    def _():
        pl.semaphore_wait(entered, far_greets * (NB - 1 - zb))

    @pl.when(owner)
    def _():
        for h in range(2):
            far_send(DB[h], far_down, d_b.at[h], "higher")

    far_send(U_B, far_up, u_b, "higher")

    def acts(r, _):
        cols = pl.ds(pl.multiple_of(r * 256, 256), 256)
        ga[:, cols] = (
            dot(cot[...], base[cols, :], 1, 1) + dot(lowout[...], down[:, cols].astype(BF), 1, 0)
        ).astype(BF)
        return 0

    lax.fori_loop(0, 2, acts, 0)

    @pl.when(owner)
    def _():
        slot = c * 2 + part
        for h in range(2):
            far_wait(DB[h], d_b.at[h])
            d_o[h] = total_of(d_b.at[h]).astype(BF)
            for k in FAR_NEAR:
                remote(d_o.at[h], d_c.at[h, slot], DC[h], near_core(k, x)).start()

            @pl.when(x == c)
            def _():
                d_c[h, slot] = d_o[h]

            @pl.when(x != c)
            def _():
                remote(d_o.at[h], d_c.at[h, slot], DC[h], pair).start()

    arrived(dec_p, DEC_PAIR)
    arrived(down_p, DOWN_PAIR)
    holds = jnp.logical_and(owner, x == c)

    for h in range(2):
        @pl.when(holds)
        def _():
            arrived(d_c.at[h, pl.ds(0, NO - 1)], DC[h])

        @pl.when(jnp.logical_not(holds))
        def _():
            arrived(d_c.at[h], DC[h])

        for j in range(2):
            cols = pl.ds(256 * j + 128 * h, 128)
            ndown[:, cols] = down[own, cols] - rate_down * (d_c[h, c * 2 + j].astype(F32) / total)
            ndown_p[:, cols] = down_p[:, cols] - rate_down * (d_c[h, oc * 2 + j].astype(F32) / total)
    low = (
        dot(ndown[...].astype(BF), dec[...], 1, 1) + dot(ndown_p[...].astype(BF), dec_p[...], 1, 1)
    ).astype(BF)
    l_y0[yy] = low[:, :256]
    for k in (2, 1, 3):
        remote(l_y0.at[yy], l_y0.at[yy], L_Y0, along_y(k)).start()
    l_x1[xh] = low[:, 256:]
    remote(l_x1.at[xh], l_x1.at[xh], L_X1, along_x).start()

    @pl.when(x == c)
    def _():
        nd_out[...] = two_rows(ndown, div(z, 4), 2 * rem(z, 4))
        nd_send[...] = jnp.concatenate([two_rows(ndown_p, div(z, 4), 2 * rem(z, 4))] * 4, axis=0)
        remote(nd_send, nd_prec, ND_PAIR, pair).start()

    far_wait(U_B, u_b)
    u_fin[c, w] = total_of(u_b).astype(BF)
    each(FAR_WIDE, wide, U_AG, lambda o: u_fin.at[c, w], u_fin.at[c, w])

    arrived(m_fin.at[c, pl.ds(0, 448)], M_AG)
    remote(m_fin.at[c], m_fin.at[c], M_PAIR2, pair).start()
    arrived(l_x1.at[0], L_X1)
    l_y1[yy] = total_of(l_x1).astype(BF)
    for k in (2, 1, 3):
        remote(l_y1.at[yy], l_y1.at[yy], L_Y1, along_y(k)).start()
    arrived(l_y0.at[pl.ds(0, 3)], L_Y0)
    l_x0[xh] = total_of(l_y0).astype(BF)
    remote(l_x0.at[xh], l_x0.at[xh], L_X0, along_x).start()

    arrived(m_fin.at[oc], M_PAIR2)
    cp_m = load(m_fin, m_h, O_M)

    @pl.when(x != c)
    def _():
        arrived(nd_prec, ND_PAIR)
        nd_out[...] = nd_prec[0:2, :]

    arrived(u_fin.at[c, pl.ds(0, NW - 1)], U_AG)
    remote(u_fin.at[c], u_fin.at[c], U_PAIR2, pair).start()

    arrived(l_x0.at[0], L_X0)
    l_fin[own, :256] = total_of(l_x0).astype(BF)
    arrived(l_y1.at[pl.ds(0, 3)], L_Y1)
    l_fin[own, 256:] = total_of(l_y1).astype(BF)
    remote(l_fin.at[own], l_fin.at[own], L_PAIR2, pair).start()

    arrived(u_fin.at[oc], U_PAIR2)
    for i in range(4):
        for j in range(NC):
            rows, cols = pl.ds(16 * i, 16), pl.ds(128 * j, 128)
            grad = u_fin[i // 2, (i % 2) * NC + j].astype(F32) / total
            new = upt[rows, cols] - rate_up * grad
            upt[rows, cols] = new
            nupt16[rows, cols] = new.astype(BF)
    first = d * 32 + t * 2
    nup[...] = upt[:, pl.ds(pl.multiple_of(div(first, 128) * 128, 128), 128)].T
    nu_out[...] = two_rows(nup, div(rem(first, 128), 8), rem(first, 8))

    arrived(l_fin.at[own], L_PAIR2)

    m_part = m_fin.at[c, pl.ds(0, 448)]
    for ref, i in (
        (u_send, U_PAIR), (u_rs.at[pl.ds(0, NW - 1)], U_RS),
        (u_a.at[pl.ds(0, GZ - 1)], U_A), (u_b.at[pl.ds(0, NB - 1)], U_B),
        (u_fin.at[c, pl.ds(0, NW - 1)], U_AG), (u_fin.at[c], U_PAIR2), (m_send, M_PAIR),
        (m_rs.at[pl.ds(0, NC - 1)], M_RS), (m_part, M_AG), (m_fin.at[c], M_PAIR2),
        (dec, DEC_PAIR), (down.at[theirs], DOWN_PAIR), (l_y0.at[pl.ds(0, 3)], L_Y0),
        (l_x0.at[0], L_X0), (l_x1.at[0], L_X1), (l_y1.at[pl.ds(0, 3)], L_Y1), (l_fin.at[own], L_PAIR2),
    ):
        sent(ref, i)

    for h in range(2):
        @pl.when(owner)
        def _():
            sent(td_send.at[h, pl.ds(0, NO - 1)], DA[h])
            sent(d_b.at[h, pl.ds(0, NB - 1)], DB[h])

            @pl.when(x == c)
            def _():
                sent(d_a.at[h, pl.ds(0, NA - 1)], DC[h])

            @pl.when(x != c)
            def _():
                sent(d_a.at[h], DC[h])

        @pl.when(jnp.logical_not(owner))
        def _():
            sent(td_send.at[h], DA[h])

    @pl.when(x == c)
    def _():
        sent(nd_send, ND_PAIR)


    cp_m.wait()


def finish_kernel(m_ref, ld_ref, nut_ref, ga_ref, nd_ref, nu_ref, dec_h, ga_h, nd_h, nu_h, dec_v, sem):
    small = [
        pltpu.make_async_copy(ref, out, sem.at[4 + i])
        for i, (ref, out) in enumerate(((ga_ref, ga_h), (nd_ref, nd_h), (nu_ref, nu_h)))
    ]
    for cp in small:
        cp.start()
    parts = []
    for r in range(4):
        rows = slice(128 * r, 128 * r + 128)
        corr = dot(ld_ref[:, rows], nut_ref[...], 0, 0)
        for h in range(2):
            cols = slice(512 * h, 512 * h + 512)
            dec_v[rows, cols] = (m_ref[h, rows, :].astype(F32) + corr[:, cols]).astype(BF)
        cp = pltpu.make_async_copy(dec_v.at[rows], dec_h.at[rows], sem.at[r])
        cp.start()
        parts.append(cp)
    for cp in parts + small:
        cp.wait()


def body(learn_acts, cotangent, base_weight, down_factor, up_factor, decode_acts):
    any_ = pl.BlockSpec(memory_space=pl.ANY)
    hbm = pl.BlockSpec(memory_space=pltpu.HBM)
    vmem = pl.BlockSpec(memory_space=pltpu.VMEM)
    V = pltpu.VMEM
    sds = jax.ShapeDtypeStruct
    ga, nd, nu, nut, ld, m = pl.pallas_call(
        comm_kernel,
        out_shape=(
            sds((512, 512), BF), sds((2, 512), F32), sds((2, 64), F32),
            sds((64, 1024), BF), sds((64, 512), BF), sds((2, 512, 512), BF),
        ),
        in_specs=[hbm] * 6,
        out_specs=(vmem,) * 5 + (any_,),
        scratch_shapes=[
            V((512, 512), BF), V((512, 1024), BF), V((512, 1024), BF), V((64, 512), F32),
            V((512, 512), BF), V((512, 512), BF), V((32, 512), F32),
            V((512, 64), BF), V((64, 512), F32), V((2, NO, 32, 128), BF), V((2, NA, 32, 128), BF),
            V((2, NB, 32, 128), BF), V((2, 32, 128), BF), V((2, NO, 32, 128), BF), V((32, 512), F32),
            V((32, 512), F32), V((8, 512), F32), V((8, 512), F32),
            V((32, 512), BF), V((32, 512), BF), V((NW, 16, 128), BF), V((NW, 16, 128), BF),
            V((GZ, 16, 128), BF), V((NB, 16, 128), BF), V((2, NW, 16, 128), BF),
            V((64, 1024), F32), V((128, 64), F32),
            V((512, 512), BF), V((512, 512), F32), V((512, 512), BF), V((NC, 64, 512), BF),
            V((NC, 64, 512), BF), V((2, 512, 512), BF), V((4, 32, 256), BF),
            V((2, 32, 256), BF), V((2, 32, 256), BF), V((4, 32, 256), BF),
            pltpu.SemaphoreType.DMA((24,)), pltpu.SemaphoreType.DMA((24,)),
            pltpu.SemaphoreType.DMA((21, NB)),
            pltpu.SemaphoreType.DMA((7,)), pltpu.SemaphoreType.REGULAR,
        ],
        compiler_params=pltpu.CompilerParams(
            collective_id=0, has_side_effects=True, vmem_limit_bytes=48 * 1024 * 1024
        ),
        name="adapter_step",
    )(*(
        pltpu.with_memory_space_constraint(arg, pltpu.HBM)
        for arg in (
            learn_acts, cotangent, base_weight, down_factor, up_factor.T, decode_acts
        )
    ))
    decoded, ga, nd, nu = pl.pallas_call(
        finish_kernel,
        out_shape=(
            sds((512, 1024), BF), sds((512, 512), BF), sds((2, 512), F32), sds((2, 64), F32),
        ),
        in_specs=[vmem] * 6,
        out_specs=(hbm,) * 4,
        scratch_shapes=[V((512, 1024), BF), pltpu.SemaphoreType.DMA((7,))],
        compiler_params=pltpu.CompilerParams(vmem_limit_bytes=16 * 1024 * 1024),
        name="finish",
    )(m, ld, nut, ga, nd, nu)
    return (ga, nd, nu, decoded)


def solution(mesh):
    in_specs = (
        P("dp", "tensor"),
        P("dp", None),
        P("tensor", None),
        P(None, "tensor"),
        P(),
        P("dp", "tensor"),
    )
    out_specs = (P("dp", "tensor"), P("dp", "tensor"), P(("dp", "tensor"), None), P("dp", None))
    return jax.shard_map(body, mesh=mesh, in_specs=in_specs, out_specs=out_specs, check_vma=False)
```

```python
import jax
import jax.numpy as jnp
from jax import lax
from jax.experimental import pallas as pl
from jax.experimental.pallas import tpu as pltpu
from jax.sharding import PartitionSpec as P

rate_down = 0.2
rate_up = 3.0

NZ = 16
GZ = 4
NA = 8
NB = 4
NO = 4
NC = 8
NW = 16

FAR_NEAR = (2, 6, 3, 5, 1, 7, 4)
BELOW_FIRST = (7, 3, 2, 6, 5, 1, 4)
FAR_CHIP = (3, 5, 1, 7, 4, 2, 6)
FAR_WIDE = (3, 13, 5, 11, 4, 12, 1, 15, 6, 10, 7, 9, 2, 14, 8)

BF = jnp.bfloat16
F32 = jnp.float32

(D_A, D_B, D_C, U_PAIR, U_RS, U_A, U_B, U_AG, U_PAIR2,
 M_PAIR, M_RS, M_AG, M_PAIR2, DEC_PAIR, L_Y0, L_PAIR2, DOWN_PAIR, ND_PAIR,
 D_A2, D_B2, D_C2, L_X0, L_X1, L_Y1) = range(24)
DA, DB, DC = (D_A, D_A2), (D_B, D_B2), (D_C, D_C2)
(I_COT, I_UP, I_LEARN, I_DOWN, I_DEC, I_BASE, O_M) = range(7)


def dot(a, b, ca, cb):
    return lax.dot_general(a, b, (((ca,), (cb,)), ((), ())), preferred_element_type=F32)


def div(a, b):
    return lax.div(a, jnp.int32(b))


def rem(a, b):
    return lax.rem(a, jnp.int32(b))


def comm_kernel(
    learn_h, cot_h, base_h, down_h, up_h, dec_h,
    ga, nd_out, nu_out, nupt16, l_fin, m_h,
    learn, cot, base, down, dec, dec_p, down_p,
    lowout, low_in, td_send, d_a, d_b, d_o, d_c, ndown, ndown_p, nd_send, nd_prec,
    u_send, u_prec, u_sum, u_rs, u_a, u_b, u_fin, upt, nup,
    m_send, m_keep, m_prec, m_sum, m_rs, m_fin, l_y0, l_x0, l_x1, l_y1,
    ssem, rsem, rfar, lsem, entered,
):
    d = lax.axis_index("dp")
    t = lax.axis_index("tensor")
    x = div(d, NZ)
    z = rem(d, NZ)
    zb = div(z, GZ)
    za = rem(z, GZ)
    a = x * GZ + za
    q = div(t, 2)
    c = rem(t, 2)
    oc = 1 - c
    yy = div(q, 2)
    xh = rem(q, 2)
    w = x * NC + q
    total = 16384.0

    def load(src, dst, i):
        cp = pltpu.make_async_copy(src, dst, lsem.at[i])
        cp.start()
        return cp

    cp_down = load(down_h, down, I_DOWN)
    cp_learn = load(learn_h, learn, I_LEARN)
    cp_up = load(up_h, upt, I_UP)
    cp_cot = load(cot_h, cot, I_COT)
    cp_dec = load(dec_h, dec, I_DEC)
    cp_base = load(base_h, base, I_BASE)

    def first_owner(group):
        return jnp.where(group == 0, 0, 1)

    part = za - first_owner(zb)
    owner = jnp.logical_or(part == 0, part == 1)
    mine = x * 2 + part

    def near(k):
        other = rem(a + k, NA)
        return other, {"dp": div(other, GZ) * NZ + zb * GZ + rem(other, GZ), "tensor": t}

    def near_core(k, core):
        return {"dp": near(k)[1]["dp"], "tensor": q * 2 + core}

    def owner_of(o):
        at = first_owner(zb) + o % 2
        return (o // 2) * GZ + at, {"dp": (o // 2) * NZ + zb * GZ + at, "tensor": t}

    def column(group, at):
        return {"dp": x * NZ + group * GZ + at, "tensor": t}

    def far_down(k):
        return column(k, first_owner(k) + part)

    def far_up(k):
        opposite = jnp.logical_or(zb == k + 2, zb == k - 2)
        return column(k, jnp.where(opposite, GZ - 1 - za, za))

    def wide(k):
        other = rem(w + k, NW)
        return other, {"dp": div(other, NC) * NZ + z, "tensor": rem(other, NC) * 2 + c}

    def above(k):
        return {"dp": x * NZ + zb * GZ + rem(za + k, GZ), "tensor": t}

    def along_y(k):
        return {"dp": d, "tensor": rem(yy + k, 4) * 4 + xh * 2 + c}

    along_x = {"dp": d, "tensor": yy * 4 + (1 - xh) * 2 + c}

    def chip(k):
        other = rem(q + k, NC)
        return other, {"dp": d, "tensor": other * 2 + c}

    pair = {"dp": d, "tensor": q * 2 + oc}

    barrier = pltpu.get_barrier_semaphore()

    def greet(dev):
        pl.semaphore_signal(barrier, inc=1, device_id=dev, device_id_type=pl.DeviceIdType.MESH)

    def hello_near(k, _):
        for core in range(2):
            greet(near_core(k, core))
        return 0

    def hello_wide(k, _):
        greet(wide(k)[1])
        return 0

    for k in FAR_NEAR:
        hello_near(k, 0)
    for k in FAR_WIDE:
        hello_wide(k, 0)
    greet(pair)
    for k in range(1, NB):
        @pl.when(zb < k)
        def _():
            greet(far_up(k))

        @pl.when(jnp.logical_and(zb < k, owner))
        def _():
            greet(far_down(k))

    def remote(src, dst, i, dev):
        return pltpu.make_async_remote_copy(
            src_ref=src, dst_ref=dst, send_sem=ssem.at[i], recv_sem=rsem.at[i],
            device_id=dev, device_id_type=pl.DeviceIdType.MESH,
        )

    def arrived(ref, i):
        remote(ref, ref, i, pair).wait_recv()

    def sent(ref, i):
        remote(ref, ref, i, pair).wait_send()

    def each(order, place, i, src, dst):
        def step(k, _):
            other, dev = place(k)
            remote(src(other), dst, i, dev).start()
            return 0
        for k in order:
            step(k, 0)

    def send_far(i, dev, buf, k):
        pltpu.make_async_remote_copy(
            src_ref=buf.at[zb], dst_ref=buf.at[zb], send_sem=ssem.at[i],
            recv_sem=rfar.at[i, zb], device_id=dev(k), device_id_type=pl.DeviceIdType.MESH,
        ).start()

    def far_arrived(i, buf, k):
        pltpu.make_async_remote_copy(
            src_ref=buf.at[k], dst_ref=buf.at[k], send_sem=ssem.at[i],
            recv_sem=rfar.at[i, k], device_id=pair, device_id_type=pl.DeviceIdType.MESH,
        ).wait_recv()

    def far_send(i, dev, buf, wanted):
        for k in range(NB):
            @pl.when(k > zb if wanted == "higher" else k < zb)
            def _():
                send_far(i, dev, buf, k)

    def far_wait(i, buf):
        for step in range(1, NB):
            far_arrived(i, buf, rem(zb + step, NB))

    def total_of(ref):
        acc = ref[0].astype(F32)
        for k in range(1, ref.shape[0]):
            acc = acc + ref[k].astype(F32)
        return acc

    def two_rows(ref, block, first):
        rows = ref[pl.ds(pl.multiple_of(block * 8, 8), 8), :]
        at = lax.broadcasted_iota(jnp.int32, rows.shape, 0)
        picked = [
            jnp.sum(jnp.where(at == first + k, rows, 0.0), axis=0, keepdims=True) for k in range(2)
        ]
        return jnp.concatenate(picked, axis=0)

    cp_down.wait()
    cp_learn.wait()
    low_in[...] = dot(down[...].astype(BF), learn[...], 1, 1)
    own = pl.ds(pl.multiple_of(c * 32, 32), 32)
    theirs = pl.ds(pl.multiple_of(oc * 32, 32), 32)
    u_send[...] = low_in[theirs, :].astype(BF)
    cp_up.wait()
    cp_cot.wait()
    lowout[...] = dot(cot[...], upt[...].astype(BF), 1, 1).astype(BF)
    term = dot(lowout[...], learn[...], 0, 0).astype(BF)
    for k in range(NO):
        i, j = k // 2, k % 2
        for h in range(2):
            td_send[h, k] = term[32 * i:32 * i + 32, 256 * j + 128 * h:256 * j + 128 * h + 128]

    far_greets = 1 + owner.astype(jnp.int32)
    pl.semaphore_wait(barrier, 2 * (NA - 1) + (NW - 1) + 1 + far_greets * zb)

    remote(u_send, u_prec, U_PAIR, pair).start()

    for h in range(2):
        for o in range(NO):
            place, dev = owner_of(o)

            @pl.when(place != a)
            def _():
                remote(td_send.at[h, o], d_a.at[h, a], DA[h], dev).start()

    for k in range(NB - 1):
        @pl.when(k < zb)
        def _():
            pl.semaphore_signal(
                entered, inc=1, device_id=far_up(k), device_id_type=pl.DeviceIdType.MESH
            )

        @pl.when(jnp.logical_and(k < zb, owner))
        def _():
            pl.semaphore_signal(
                entered, inc=1, device_id=far_down(k), device_id_type=pl.DeviceIdType.MESH
            )

    @pl.when(owner)
    def _():
        for h in range(2):
            d_a[h, a] = td_send[h, mine]

    arrived(u_prec, U_PAIR)
    pair_in = (low_in[own, :] + u_prec[...].astype(F32)).astype(BF)
    term_up = dot(pair_in, cot[...], 1, 0).astype(BF)
    for i in range(2):
        for j in range(NC):
            u_sum[i * NC + j] = term_up[16 * i:16 * i + 16, 128 * j:128 * j + 128]
    u_rs[w] = u_sum[w]
    each(FAR_WIDE, wide, U_RS, lambda o: u_sum.at[o], u_rs.at[w])

    cp_dec.wait()
    cp_base.wait()

    def other_half(r, _):
        to = pl.ds(pl.multiple_of(r * 256, 256), 256)
        cols = pl.ds(pl.multiple_of(oc * 512 + r * 256, 256), 256)
        m_send[:, to] = dot(dec[...], base[:, cols], 1, 0).astype(BF)
        return 0

    def own_half(r, _):
        to = pl.ds(pl.multiple_of(r * 256, 256), 256)
        cols = pl.ds(pl.multiple_of(c * 512 + r * 256, 256), 256)
        m_keep[:, to] = dot(dec[...], base[:, cols], 1, 0)
        return 0

    lax.fori_loop(0, 2, other_half, 0)
    remote(m_send, m_prec, M_PAIR, pair).start()

    remote(dec, dec_p, DEC_PAIR, pair).start()
    remote(down.at[theirs], down_p, DOWN_PAIR, pair).start()

    lax.fori_loop(0, 2, own_half, 0)
    @pl.when(owner)
    def _():
        for h in range(2):
            arrived(d_a.at[h, pl.ds(0, NA - 1)], DA[h])
            d_b[h, zb] = total_of(d_a.at[h]).astype(BF)
            far_send(DB[h], far_down, d_b.at[h], "lower")

    arrived(m_prec, M_PAIR)

    def add_half(r, _):
        rows = pl.ds(pl.multiple_of(r * 64, 64), 64)
        m_sum[r] = (m_keep[rows, :] + m_prec[rows, :].astype(F32)).astype(BF)
        return 0

    lax.fori_loop(0, NC, add_half, 0)
    m_rs[q] = m_sum[q]

    each(FAR_CHIP, chip, M_RS, lambda o: m_sum.at[o], m_rs.at[q])

    arrived(u_rs.at[pl.ds(0, NW - 1)], U_RS)
    u_a[za] = total_of(u_rs).astype(BF)
    for k in range(1, GZ):
        remote(u_a.at[za], u_a.at[za], U_A, above(k)).start()

    arrived(u_a.at[pl.ds(0, GZ - 1)], U_A)
    u_b[zb] = total_of(u_a).astype(BF)
    far_send(U_B, far_up, u_b, "lower")

    my_rows = pl.ds(pl.multiple_of(q * 64, 64), 64)
    arrived(m_rs.at[pl.ds(0, NC - 1)], M_RS)
    m_fin[c, my_rows, :] = total_of(m_rs).astype(BF)
    each(FAR_CHIP, chip, M_AG, lambda o: m_fin.at[c, my_rows], m_fin.at[c, my_rows])

    @pl.when(zb < NB - 1)
    def _():
        pl.semaphore_wait(entered, far_greets * (NB - 1 - zb))

    @pl.when(owner)
    def _():
        for h in range(2):
            far_send(DB[h], far_down, d_b.at[h], "higher")

    far_send(U_B, far_up, u_b, "higher")

    def acts(r, _):
        cols = pl.ds(pl.multiple_of(r * 256, 256), 256)
        ga[:, cols] = (
            dot(cot[...], base[cols, :], 1, 1) + dot(lowout[...], down[:, cols].astype(BF), 1, 0)
        ).astype(BF)
        return 0

    lax.fori_loop(0, 2, acts, 0)

    @pl.when(owner)
    def _():
        slot = c * 2 + part
        for h in range(2):
            far_wait(DB[h], d_b.at[h])
            d_o[h] = total_of(d_b.at[h]).astype(BF)
            @pl.when(x == c)
            def _():
                d_c[h, slot] = d_o[h]

            @pl.when(x != c)
            def _():
                remote(d_o.at[h], d_c.at[h, slot], DC[h], pair).start()

            for k in BELOW_FIRST:
                remote(d_o.at[h], d_c.at[h, slot], DC[h], near_core(k, x)).start()

    arrived(dec_p, DEC_PAIR)
    arrived(down_p, DOWN_PAIR)
    holds = jnp.logical_and(owner, x == c)

    for h in range(2):
        @pl.when(holds)
        def _():
            arrived(d_c.at[h, pl.ds(0, NO - 1)], DC[h])

        @pl.when(jnp.logical_not(holds))
        def _():
            arrived(d_c.at[h], DC[h])

        for j in range(2):
            cols = pl.ds(256 * j + 128 * h, 128)
            ndown[:, cols] = down[own, cols] - rate_down * (d_c[h, c * 2 + j].astype(F32) / total)
            ndown_p[:, cols] = down_p[:, cols] - rate_down * (d_c[h, oc * 2 + j].astype(F32) / total)
    low = (
        dot(ndown[...].astype(BF), dec[...], 1, 1) + dot(ndown_p[...].astype(BF), dec_p[...], 1, 1)
    ).astype(BF)
    l_y0[yy] = low[:, :256]
    for k in (2, 1, 3):
        remote(l_y0.at[yy], l_y0.at[yy], L_Y0, along_y(k)).start()
    l_x1[xh] = low[:, 256:]
    remote(l_x1.at[xh], l_x1.at[xh], L_X1, along_x).start()

    @pl.when(x == c)
    def _():
        nd_out[...] = two_rows(ndown, div(z, 4), 2 * rem(z, 4))
        nd_send[...] = jnp.concatenate([two_rows(ndown_p, div(z, 4), 2 * rem(z, 4))] * 4, axis=0)
        remote(nd_send, nd_prec, ND_PAIR, pair).start()

    far_wait(U_B, u_b)
    u_fin[c, w] = total_of(u_b).astype(BF)
    each(FAR_WIDE, wide, U_AG, lambda o: u_fin.at[c, w], u_fin.at[c, w])

    arrived(m_fin.at[c, pl.ds(0, 448)], M_AG)
    remote(m_fin.at[c], m_fin.at[c], M_PAIR2, pair).start()
    arrived(l_x1.at[0], L_X1)
    l_y1[yy] = total_of(l_x1).astype(BF)
    for k in (2, 1, 3):
        remote(l_y1.at[yy], l_y1.at[yy], L_Y1, along_y(k)).start()
    arrived(l_y0.at[pl.ds(0, 3)], L_Y0)
    l_x0[xh] = total_of(l_y0).astype(BF)
    remote(l_x0.at[xh], l_x0.at[xh], L_X0, along_x).start()

    arrived(m_fin.at[oc], M_PAIR2)
    cp_m = load(m_fin, m_h, O_M)

    m_part = m_fin.at[c, pl.ds(0, 448)]
    for ref, i in (
        (u_send, U_PAIR), (u_rs.at[pl.ds(0, NW - 1)], U_RS),
        (u_a.at[pl.ds(0, GZ - 1)], U_A), (u_b.at[pl.ds(0, NB - 1)], U_B), (m_send, M_PAIR),
        (m_rs.at[pl.ds(0, NC - 1)], M_RS), (m_part, M_AG),
        (dec, DEC_PAIR), (down.at[theirs], DOWN_PAIR),
    ):
        sent(ref, i)

    for h in range(2):
        @pl.when(owner)
        def _():
            sent(td_send.at[h, pl.ds(0, NO - 1)], DA[h])
            sent(d_b.at[h, pl.ds(0, NB - 1)], DB[h])

            @pl.when(x == c)
            def _():
                sent(d_a.at[h, pl.ds(0, NA - 1)], DC[h])

            @pl.when(x != c)
            def _():
                sent(d_a.at[h], DC[h])

        @pl.when(jnp.logical_not(owner))
        def _():
            sent(td_send.at[h], DA[h])

    @pl.when(x == c)
    def _():
        sent(nd_send, ND_PAIR)


    @pl.when(x != c)
    def _():
        arrived(nd_prec, ND_PAIR)
        nd_out[...] = nd_prec[0:2, :]

    arrived(u_fin.at[c, pl.ds(0, NW - 1)], U_AG)
    remote(u_fin.at[c], u_fin.at[c], U_PAIR2, pair).start()

    arrived(l_x0.at[0], L_X0)
    l_fin[own, :256] = total_of(l_x0).astype(BF)
    arrived(l_y1.at[pl.ds(0, 3)], L_Y1)
    l_fin[own, 256:] = total_of(l_y1).astype(BF)
    remote(l_fin.at[own], l_fin.at[own], L_PAIR2, pair).start()

    arrived(u_fin.at[oc], U_PAIR2)
    for i in range(4):
        for j in range(NC):
            rows, cols = pl.ds(16 * i, 16), pl.ds(128 * j, 128)
            grad = u_fin[i // 2, (i % 2) * NC + j].astype(F32) / total
            new = upt[rows, cols] - rate_up * grad
            upt[rows, cols] = new
            nupt16[rows, cols] = new.astype(BF)
    first = d * 32 + t * 2
    nup[...] = upt[:, pl.ds(pl.multiple_of(div(first, 128) * 128, 128), 128)].T
    nu_out[...] = two_rows(nup, div(rem(first, 128), 8), rem(first, 8))

    arrived(l_fin.at[own], L_PAIR2)

    for ref, i in (
        (u_fin.at[c, pl.ds(0, NW - 1)], U_AG), (u_fin.at[c], U_PAIR2), (m_fin.at[c], M_PAIR2),
        (l_y0.at[pl.ds(0, 3)], L_Y0), (l_x0.at[0], L_X0), (l_x1.at[0], L_X1),
        (l_y1.at[pl.ds(0, 3)], L_Y1), (l_fin.at[own], L_PAIR2),
    ):
        sent(ref, i)
    cp_m.wait()


def finish_kernel(m_ref, ld_ref, nut_ref, ga_ref, nd_ref, nu_ref, dec_h, ga_h, nd_h, nu_h, dec_v, sem):
    small = [
        pltpu.make_async_copy(ref, out, sem.at[4 + i])
        for i, (ref, out) in enumerate(((ga_ref, ga_h), (nd_ref, nd_h), (nu_ref, nu_h)))
    ]
    for cp in small:
        cp.start()
    parts = []
    for r in range(4):
        rows = slice(128 * r, 128 * r + 128)
        corr = dot(ld_ref[:, rows], nut_ref[...], 0, 0)
        for h in range(2):
            cols = slice(512 * h, 512 * h + 512)
            dec_v[rows, cols] = (m_ref[h, rows, :].astype(F32) + corr[:, cols]).astype(BF)
        cp = pltpu.make_async_copy(dec_v.at[rows], dec_h.at[rows], sem.at[r])
        cp.start()
        parts.append(cp)
    for cp in parts + small:
        cp.wait()


def body(learn_acts, cotangent, base_weight, down_factor, up_factor, decode_acts):
    any_ = pl.BlockSpec(memory_space=pl.ANY)
    hbm = pl.BlockSpec(memory_space=pltpu.HBM)
    vmem = pl.BlockSpec(memory_space=pltpu.VMEM)
    V = pltpu.VMEM
    sds = jax.ShapeDtypeStruct
    ga, nd, nu, nut, ld, m = pl.pallas_call(
        comm_kernel,
        out_shape=(
            sds((512, 512), BF), sds((2, 512), F32), sds((2, 64), F32),
            sds((64, 1024), BF), sds((64, 512), BF), sds((2, 512, 512), BF),
        ),
        in_specs=[hbm] * 6,
        out_specs=(vmem,) * 5 + (any_,),
        scratch_shapes=[
            V((512, 512), BF), V((512, 1024), BF), V((512, 1024), BF), V((64, 512), F32),
            V((512, 512), BF), V((512, 512), BF), V((32, 512), F32),
            V((512, 64), BF), V((64, 512), F32), V((2, NO, 32, 128), BF), V((2, NA, 32, 128), BF),
            V((2, NB, 32, 128), BF), V((2, 32, 128), BF), V((2, NO, 32, 128), BF), V((32, 512), F32),
            V((32, 512), F32), V((8, 512), F32), V((8, 512), F32),
            V((32, 512), BF), V((32, 512), BF), V((NW, 16, 128), BF), V((NW, 16, 128), BF),
            V((GZ, 16, 128), BF), V((NB, 16, 128), BF), V((2, NW, 16, 128), BF),
            V((64, 1024), F32), V((128, 64), F32),
            V((512, 512), BF), V((512, 512), F32), V((512, 512), BF), V((NC, 64, 512), BF),
            V((NC, 64, 512), BF), V((2, 512, 512), BF), V((4, 32, 256), BF),
            V((2, 32, 256), BF), V((2, 32, 256), BF), V((4, 32, 256), BF),
            pltpu.SemaphoreType.DMA((24,)), pltpu.SemaphoreType.DMA((24,)),
            pltpu.SemaphoreType.DMA((21, NB)),
            pltpu.SemaphoreType.DMA((7,)), pltpu.SemaphoreType.REGULAR,
        ],
        compiler_params=pltpu.CompilerParams(
            collective_id=0, has_side_effects=True, vmem_limit_bytes=48 * 1024 * 1024
        ),
        name="adapter_step",
    )(*(
        pltpu.with_memory_space_constraint(arg, pltpu.HBM)
        for arg in (
            learn_acts, cotangent, base_weight, down_factor, up_factor.T, decode_acts
        )
    ))
    decoded, ga, nd, nu = pl.pallas_call(
        finish_kernel,
        out_shape=(
            sds((512, 1024), BF), sds((512, 512), BF), sds((2, 512), F32), sds((2, 64), F32),
        ),
        in_specs=[vmem] * 6,
        out_specs=(hbm,) * 4,
        scratch_shapes=[V((512, 1024), BF), pltpu.SemaphoreType.DMA((7,))],
        compiler_params=pltpu.CompilerParams(vmem_limit_bytes=16 * 1024 * 1024),
        name="finish",
    )(m, ld, nut, ga, nd, nu)
    return (ga, nd, nu, decoded)


def solution(mesh):
    in_specs = (
        P("dp", "tensor"),
        P("dp", None),
        P("tensor", None),
        P(None, "tensor"),
        P(),
        P("dp", "tensor"),
    )
    out_specs = (P("dp", "tensor"), P("dp", "tensor"), P(("dp", "tensor"), None), P("dp", None))
    return jax.shard_map(body, mesh=mesh, in_specs=in_specs, out_specs=out_specs, check_vma=False)
```

```python
import jax
import jax.numpy as jnp
from jax import lax
from jax.experimental import pallas as pl
from jax.experimental.pallas import tpu as pltpu
from jax.sharding import PartitionSpec as P

rate_down = 0.2
rate_up = 3.0

NZ = 16
GZ = 4
NA = 8
NB = 4
NO = 4
NC = 8
NW = 16

FAR_NEAR = (2, 6, 3, 5, 1, 7, 4)
BELOW_FIRST = (7, 3, 2, 6, 5, 1, 4)
FAR_CHIP = (3, 5, 1, 7, 4, 2, 6)
FAR_WIDE = (3, 13, 5, 11, 4, 12, 1, 15, 6, 10, 7, 9, 2, 14, 8)

BF = jnp.bfloat16
F32 = jnp.float32

(D_A, D_B, D_C, U_PAIR, U_RS, U_A, U_B, U_AG, U_PAIR2,
 M_PAIR, M_RS, M_AG, M_PAIR2, DEC_PAIR, L_Y0, L_PAIR2, DOWN_PAIR, ND_PAIR,
 D_A2, D_B2, D_C2, L_X0, L_X1, L_Y1) = range(24)
DA, DB, DC = (D_A, D_A2), (D_B, D_B2), (D_C, D_C2)
(I_COT, I_UP, I_LEARN, I_DOWN, I_DEC, I_BASE, O_M) = range(7)


def dot(a, b, ca, cb):
    return lax.dot_general(a, b, (((ca,), (cb,)), ((), ())), preferred_element_type=F32)


def div(a, b):
    return lax.div(a, jnp.int32(b))


def rem(a, b):
    return lax.rem(a, jnp.int32(b))


def comm_kernel(
    learn_h, cot_h, base_h, down_h, up_h, dec_h,
    ga, nd_out, nu_out, nupt16, l_fin, m_h,
    learn, cot, base, down, dec, dec_p, down_p,
    lowout, low_in, td_send, d_a, d_b, d_o, d_c, ndown, ndown_p, nd_send, nd_prec,
    u_send, u_prec, u_sum, u_rs, u_a, u_b, u_fin, upt, nup,
    m_send, m_keep, m_prec, m_sum, m_rs, m_fin, l_y0, l_x0, l_x1, l_y1,
    ssem, rsem, rfar, lsem, entered,
):
    d = lax.axis_index("dp")
    t = lax.axis_index("tensor")
    x = div(d, NZ)
    z = rem(d, NZ)
    zb = div(z, GZ)
    za = rem(z, GZ)
    a = x * GZ + za
    q = div(t, 2)
    c = rem(t, 2)
    oc = 1 - c
    yy = div(q, 2)
    xh = rem(q, 2)
    w = x * NC + q
    total = 16384.0

    def load(src, dst, i):
        cp = pltpu.make_async_copy(src, dst, lsem.at[i])
        cp.start()
        return cp

    cp_down = load(down_h, down, I_DOWN)
    cp_learn = load(learn_h, learn, I_LEARN)
    cp_up = load(up_h, upt, I_UP)
    cp_cot = load(cot_h, cot, I_COT)
    cp_dec = load(dec_h, dec, I_DEC)
    cp_base = load(base_h, base, I_BASE)

    def first_owner(group):
        return jnp.where(group == 0, 0, 1)

    part = za - first_owner(zb)
    owner = jnp.logical_or(part == 0, part == 1)
    mine = x * 2 + part

    def near(k):
        other = rem(a + k, NA)
        return other, {"dp": div(other, GZ) * NZ + zb * GZ + rem(other, GZ), "tensor": t}

    def near_core(k, core):
        return {"dp": near(k)[1]["dp"], "tensor": q * 2 + core}

    def owner_of(o):
        at = first_owner(zb) + o % 2
        return (o // 2) * GZ + at, {"dp": (o // 2) * NZ + zb * GZ + at, "tensor": t}

    def column(group, at):
        return {"dp": x * NZ + group * GZ + at, "tensor": t}

    def far_down(k):
        return column(k, first_owner(k) + part)

    def far_up(k):
        opposite = jnp.logical_or(zb == k + 2, zb == k - 2)
        return column(k, jnp.where(opposite, GZ - 1 - za, za))

    def wide(k):
        other = rem(w + k, NW)
        return other, {"dp": div(other, NC) * NZ + z, "tensor": rem(other, NC) * 2 + c}

    def above(k):
        return {"dp": x * NZ + zb * GZ + rem(za + k, GZ), "tensor": t}

    def along_y(k):
        return {"dp": d, "tensor": rem(yy + k, 4) * 4 + xh * 2 + c}

    along_x = {"dp": d, "tensor": yy * 4 + (1 - xh) * 2 + c}

    def chip(k):
        other = rem(q + k, NC)
        return other, {"dp": d, "tensor": other * 2 + c}

    pair = {"dp": d, "tensor": q * 2 + oc}

    barrier = pltpu.get_barrier_semaphore()

    def greet(dev):
        pl.semaphore_signal(barrier, inc=1, device_id=dev, device_id_type=pl.DeviceIdType.MESH)

    def hello_near(k, _):
        for core in range(2):
            greet(near_core(k, core))
        return 0

    def hello_wide(k, _):
        greet(wide(k)[1])
        return 0

    for k in FAR_NEAR:
        hello_near(k, 0)
    for k in FAR_WIDE:
        hello_wide(k, 0)
    greet(pair)
    for k in range(1, NB):
        @pl.when(zb < k)
        def _():
            greet(far_up(k))

        @pl.when(jnp.logical_and(zb < k, owner))
        def _():
            greet(far_down(k))

    def remote(src, dst, i, dev):
        return pltpu.make_async_remote_copy(
            src_ref=src, dst_ref=dst, send_sem=ssem.at[i], recv_sem=rsem.at[i],
            device_id=dev, device_id_type=pl.DeviceIdType.MESH,
        )

    def arrived(ref, i):
        remote(ref, ref, i, pair).wait_recv()

    def sent(ref, i):
        remote(ref, ref, i, pair).wait_send()

    def each(order, place, i, src, dst):
        def step(k, _):
            other, dev = place(k)
            remote(src(other), dst, i, dev).start()
            return 0
        for k in order:
            step(k, 0)

    def send_far(i, dev, buf, k):
        pltpu.make_async_remote_copy(
            src_ref=buf.at[zb], dst_ref=buf.at[zb], send_sem=ssem.at[i],
            recv_sem=rfar.at[i, zb], device_id=dev(k), device_id_type=pl.DeviceIdType.MESH,
        ).start()

    def far_arrived(i, buf, k):
        pltpu.make_async_remote_copy(
            src_ref=buf.at[k], dst_ref=buf.at[k], send_sem=ssem.at[i],
            recv_sem=rfar.at[i, k], device_id=pair, device_id_type=pl.DeviceIdType.MESH,
        ).wait_recv()

    def far_send(i, dev, buf, wanted):
        for k in range(NB):
            @pl.when(k > zb if wanted == "higher" else k < zb)
            def _():
                send_far(i, dev, buf, k)

    def far_wait(i, buf):
        for step in range(1, NB):
            far_arrived(i, buf, rem(zb + step, NB))

    def total_of(ref):
        acc = ref[0].astype(F32)
        for k in range(1, ref.shape[0]):
            acc = acc + ref[k].astype(F32)
        return acc

    def two_rows(ref, block, first):
        rows = ref[pl.ds(pl.multiple_of(block * 8, 8), 8), :]
        at = lax.broadcasted_iota(jnp.int32, rows.shape, 0)
        picked = [
            jnp.sum(jnp.where(at == first + k, rows, 0.0), axis=0, keepdims=True) for k in range(2)
        ]
        return jnp.concatenate(picked, axis=0)

    cp_down.wait()
    cp_learn.wait()
    low_in[...] = dot(down[...].astype(BF), learn[...], 1, 1)
    own = pl.ds(pl.multiple_of(c * 32, 32), 32)
    theirs = pl.ds(pl.multiple_of(oc * 32, 32), 32)
    u_send[...] = low_in[theirs, :].astype(BF)
    cp_up.wait()
    cp_cot.wait()
    lowout[...] = dot(cot[...], upt[...].astype(BF), 1, 1).astype(BF)
    term = dot(lowout[...], learn[...], 0, 0).astype(BF)
    for k in range(NO):
        i, j = k // 2, k % 2
        for h in range(2):
            td_send[h, k] = term[32 * i:32 * i + 32, 256 * j + 128 * h:256 * j + 128 * h + 128]

    far_greets = 1 + owner.astype(jnp.int32)
    pl.semaphore_wait(barrier, 2 * (NA - 1) + (NW - 1) + 1 + far_greets * zb)

    remote(u_send, u_prec, U_PAIR, pair).start()

    for h in range(2):
        for o in range(NO):
            place, dev = owner_of(o)

            @pl.when(place != a)
            def _():
                remote(td_send.at[h, o], d_a.at[h, a], DA[h], dev).start()

    for k in range(NB - 1):
        @pl.when(k < zb)
        def _():
            pl.semaphore_signal(
                entered, inc=1, device_id=far_up(k), device_id_type=pl.DeviceIdType.MESH
            )

        @pl.when(jnp.logical_and(k < zb, owner))
        def _():
            pl.semaphore_signal(
                entered, inc=1, device_id=far_down(k), device_id_type=pl.DeviceIdType.MESH
            )

    @pl.when(owner)
    def _():
        for h in range(2):
            d_a[h, a] = td_send[h, mine]

    arrived(u_prec, U_PAIR)
    pair_in = (low_in[own, :] + u_prec[...].astype(F32)).astype(BF)
    term_up = dot(pair_in, cot[...], 1, 0).astype(BF)
    for i in range(2):
        for j in range(NC):
            u_sum[i * NC + j] = term_up[16 * i:16 * i + 16, 128 * j:128 * j + 128]
    u_rs[w] = u_sum[w]
    each(FAR_WIDE, wide, U_RS, lambda o: u_sum.at[o], u_rs.at[w])

    cp_dec.wait()
    cp_base.wait()

    def other_half(r, _):
        to = pl.ds(pl.multiple_of(r * 256, 256), 256)
        cols = pl.ds(pl.multiple_of(oc * 512 + r * 256, 256), 256)
        m_send[:, to] = dot(dec[...], base[:, cols], 1, 0).astype(BF)
        return 0

    def own_half(r, _):
        to = pl.ds(pl.multiple_of(r * 256, 256), 256)
        cols = pl.ds(pl.multiple_of(c * 512 + r * 256, 256), 256)
        m_keep[:, to] = dot(dec[...], base[:, cols], 1, 0)
        return 0

    lax.fori_loop(0, 2, other_half, 0)
    remote(m_send, m_prec, M_PAIR, pair).start()

    remote(dec, dec_p, DEC_PAIR, pair).start()
    remote(down.at[theirs], down_p, DOWN_PAIR, pair).start()

    lax.fori_loop(0, 2, own_half, 0)
    @pl.when(owner)
    def _():
        for h in range(2):
            arrived(d_a.at[h, pl.ds(0, NA - 1)], DA[h])
            d_b[h, zb] = total_of(d_a.at[h]).astype(BF)
            far_send(DB[h], far_down, d_b.at[h], "lower")

    arrived(m_prec, M_PAIR)

    def add_half(r, _):
        rows = pl.ds(pl.multiple_of(r * 64, 64), 64)
        m_sum[r] = (m_keep[rows, :] + m_prec[rows, :].astype(F32)).astype(BF)
        return 0

    lax.fori_loop(0, NC, add_half, 0)
    m_rs[q] = m_sum[q]

    each(FAR_CHIP, chip, M_RS, lambda o: m_sum.at[o], m_rs.at[q])

    arrived(u_rs.at[pl.ds(0, NW - 1)], U_RS)
    u_a[za] = total_of(u_rs).astype(BF)
    for k in range(1, GZ):
        remote(u_a.at[za], u_a.at[za], U_A, above(k)).start()

    arrived(u_a.at[pl.ds(0, GZ - 1)], U_A)
    u_b[zb] = total_of(u_a).astype(BF)
    far_send(U_B, far_up, u_b, "lower")

    my_rows = pl.ds(pl.multiple_of(q * 64, 64), 64)
    arrived(m_rs.at[pl.ds(0, NC - 1)], M_RS)
    m_fin[c, my_rows, :] = total_of(m_rs).astype(BF)
    each(FAR_CHIP, chip, M_AG, lambda o: m_fin.at[c, my_rows], m_fin.at[c, my_rows])

    @pl.when(zb < NB - 1)
    def _():
        pl.semaphore_wait(entered, far_greets * (NB - 1 - zb))

    @pl.when(owner)
    def _():
        for h in range(2):
            far_send(DB[h], far_down, d_b.at[h], "higher")

    far_send(U_B, far_up, u_b, "higher")

    def acts(r, _):
        cols = pl.ds(pl.multiple_of(r * 256, 256), 256)
        ga[:, cols] = (
            dot(cot[...], base[cols, :], 1, 1) + dot(lowout[...], down[:, cols].astype(BF), 1, 0)
        ).astype(BF)
        return 0

    lax.fori_loop(0, 2, acts, 0)

    @pl.when(owner)
    def _():
        slot = c * 2 + part
        for h in range(2):
            far_wait(DB[h], d_b.at[h])
            d_o[h] = total_of(d_b.at[h]).astype(BF)
            @pl.when(x == c)
            def _():
                d_c[h, slot] = d_o[h]

            @pl.when(x != c)
            def _():
                remote(d_o.at[h], d_c.at[h, slot], DC[h], pair).start()

            for k in BELOW_FIRST:
                remote(d_o.at[h], d_c.at[h, slot], DC[h], near_core(k, x)).start()

    arrived(dec_p, DEC_PAIR)
    arrived(down_p, DOWN_PAIR)
    holds = jnp.logical_and(owner, x == c)

    low = jnp.zeros((32, 512), F32)
    for h in range(2):
        @pl.when(holds)
        def _():
            arrived(d_c.at[h, pl.ds(0, NO - 1)], DC[h])

        @pl.when(jnp.logical_not(holds))
        def _():
            arrived(d_c.at[h], DC[h])

        for j in range(2):
            cols = pl.ds(256 * j + 128 * h, 128)
            ndown[:, cols] = down[own, cols] - rate_down * (d_c[h, c * 2 + j].astype(F32) / total)
            ndown_p[:, cols] = down_p[:, cols] - rate_down * (d_c[h, oc * 2 + j].astype(F32) / total)
            low += dot(ndown[:, cols].astype(BF), dec[:, cols], 1, 1)
            low += dot(ndown_p[:, cols].astype(BF), dec_p[:, cols], 1, 1)
    low = low.astype(BF)
    l_y0[yy] = low[:, :256]
    for k in (2, 1, 3):
        remote(l_y0.at[yy], l_y0.at[yy], L_Y0, along_y(k)).start()
    l_x1[xh] = low[:, 256:]
    remote(l_x1.at[xh], l_x1.at[xh], L_X1, along_x).start()

    @pl.when(x == c)
    def _():
        nd_out[...] = two_rows(ndown, div(z, 4), 2 * rem(z, 4))
        nd_send[...] = jnp.concatenate([two_rows(ndown_p, div(z, 4), 2 * rem(z, 4))] * 4, axis=0)
        remote(nd_send, nd_prec, ND_PAIR, pair).start()

    far_wait(U_B, u_b)
    u_fin[c, w] = total_of(u_b).astype(BF)
    each(FAR_WIDE, wide, U_AG, lambda o: u_fin.at[c, w], u_fin.at[c, w])

    arrived(m_fin.at[c, pl.ds(0, 448)], M_AG)
    remote(m_fin.at[c], m_fin.at[c], M_PAIR2, pair).start()
    arrived(l_x1.at[0], L_X1)
    l_y1[yy] = total_of(l_x1).astype(BF)
    for k in (2, 1, 3):
        remote(l_y1.at[yy], l_y1.at[yy], L_Y1, along_y(k)).start()
    arrived(l_y0.at[pl.ds(0, 3)], L_Y0)
    l_x0[xh] = total_of(l_y0).astype(BF)
    remote(l_x0.at[xh], l_x0.at[xh], L_X0, along_x).start()

    arrived(m_fin.at[oc], M_PAIR2)
    cp_m = load(m_fin, m_h, O_M)

    m_part = m_fin.at[c, pl.ds(0, 448)]
    for ref, i in (
        (u_send, U_PAIR), (u_rs.at[pl.ds(0, NW - 1)], U_RS),
        (u_a.at[pl.ds(0, GZ - 1)], U_A), (u_b.at[pl.ds(0, NB - 1)], U_B), (m_send, M_PAIR),
        (m_rs.at[pl.ds(0, NC - 1)], M_RS), (m_part, M_AG),
        (dec, DEC_PAIR), (down.at[theirs], DOWN_PAIR),
    ):
        sent(ref, i)

    for h in range(2):
        @pl.when(owner)
        def _():
            sent(td_send.at[h, pl.ds(0, NO - 1)], DA[h])
            sent(d_b.at[h, pl.ds(0, NB - 1)], DB[h])

            @pl.when(x == c)
            def _():
                sent(d_a.at[h, pl.ds(0, NA - 1)], DC[h])

            @pl.when(x != c)
            def _():
                sent(d_a.at[h], DC[h])

        @pl.when(jnp.logical_not(owner))
        def _():
            sent(td_send.at[h], DA[h])

    @pl.when(x == c)
    def _():
        sent(nd_send, ND_PAIR)


    @pl.when(x != c)
    def _():
        arrived(nd_prec, ND_PAIR)
        nd_out[...] = nd_prec[0:2, :]

    arrived(u_fin.at[c, pl.ds(0, NW - 1)], U_AG)
    remote(u_fin.at[c], u_fin.at[c], U_PAIR2, pair).start()

    arrived(l_x0.at[0], L_X0)
    l_fin[own, :256] = total_of(l_x0).astype(BF)
    arrived(l_y1.at[pl.ds(0, 3)], L_Y1)
    l_fin[own, 256:] = total_of(l_y1).astype(BF)
    remote(l_fin.at[own], l_fin.at[own], L_PAIR2, pair).start()

    arrived(u_fin.at[oc], U_PAIR2)
    for i in range(4):
        for j in range(NC):
            rows, cols = pl.ds(16 * i, 16), pl.ds(128 * j, 128)
            grad = u_fin[i // 2, (i % 2) * NC + j].astype(F32) / total
            new = upt[rows, cols] - rate_up * grad
            upt[rows, cols] = new
            nupt16[rows, cols] = new.astype(BF)
    first = d * 32 + t * 2
    nup[...] = upt[:, pl.ds(pl.multiple_of(div(first, 128) * 128, 128), 128)].T
    nu_out[...] = two_rows(nup, div(rem(first, 128), 8), rem(first, 8))

    arrived(l_fin.at[own], L_PAIR2)

    for ref, i in (
        (u_fin.at[c, pl.ds(0, NW - 1)], U_AG), (u_fin.at[c], U_PAIR2), (m_fin.at[c], M_PAIR2),
        (l_y0.at[pl.ds(0, 3)], L_Y0), (l_x0.at[0], L_X0), (l_x1.at[0], L_X1),
        (l_y1.at[pl.ds(0, 3)], L_Y1), (l_fin.at[own], L_PAIR2),
    ):
        sent(ref, i)
    cp_m.wait()


def finish_kernel(m_ref, ld_ref, nut_ref, ga_ref, nd_ref, nu_ref, dec_h, ga_h, nd_h, nu_h, dec_v, sem):
    small = [
        pltpu.make_async_copy(ref, out, sem.at[4 + i])
        for i, (ref, out) in enumerate(((ga_ref, ga_h), (nd_ref, nd_h), (nu_ref, nu_h)))
    ]
    for cp in small:
        cp.start()
    parts = []
    for r in range(4):
        rows = slice(128 * r, 128 * r + 128)
        corr = dot(ld_ref[:, rows], nut_ref[...], 0, 0)
        for h in range(2):
            cols = slice(512 * h, 512 * h + 512)
            dec_v[rows, cols] = (m_ref[h, rows, :].astype(F32) + corr[:, cols]).astype(BF)
        cp = pltpu.make_async_copy(dec_v.at[rows], dec_h.at[rows], sem.at[r])
        cp.start()
        parts.append(cp)
    for cp in parts + small:
        cp.wait()


def body(learn_acts, cotangent, base_weight, down_factor, up_factor, decode_acts):
    any_ = pl.BlockSpec(memory_space=pl.ANY)
    hbm = pl.BlockSpec(memory_space=pltpu.HBM)
    vmem = pl.BlockSpec(memory_space=pltpu.VMEM)
    V = pltpu.VMEM
    sds = jax.ShapeDtypeStruct
    ga, nd, nu, nut, ld, m = pl.pallas_call(
        comm_kernel,
        out_shape=(
            sds((512, 512), BF), sds((2, 512), F32), sds((2, 64), F32),
            sds((64, 1024), BF), sds((64, 512), BF), sds((2, 512, 512), BF),
        ),
        in_specs=[hbm] * 6,
        out_specs=(vmem,) * 5 + (any_,),
        scratch_shapes=[
            V((512, 512), BF), V((512, 1024), BF), V((512, 1024), BF), V((64, 512), F32),
            V((512, 512), BF), V((512, 512), BF), V((32, 512), F32),
            V((512, 64), BF), V((64, 512), F32), V((2, NO, 32, 128), BF), V((2, NA, 32, 128), BF),
            V((2, NB, 32, 128), BF), V((2, 32, 128), BF), V((2, NO, 32, 128), BF), V((32, 512), F32),
            V((32, 512), F32), V((8, 512), F32), V((8, 512), F32),
            V((32, 512), BF), V((32, 512), BF), V((NW, 16, 128), BF), V((NW, 16, 128), BF),
            V((GZ, 16, 128), BF), V((NB, 16, 128), BF), V((2, NW, 16, 128), BF),
            V((64, 1024), F32), V((128, 64), F32),
            V((512, 512), BF), V((512, 512), F32), V((512, 512), BF), V((NC, 64, 512), BF),
            V((NC, 64, 512), BF), V((2, 512, 512), BF), V((4, 32, 256), BF),
            V((2, 32, 256), BF), V((2, 32, 256), BF), V((4, 32, 256), BF),
            pltpu.SemaphoreType.DMA((24,)), pltpu.SemaphoreType.DMA((24,)),
            pltpu.SemaphoreType.DMA((21, NB)),
            pltpu.SemaphoreType.DMA((7,)), pltpu.SemaphoreType.REGULAR,
        ],
        compiler_params=pltpu.CompilerParams(
            collective_id=0, has_side_effects=True, vmem_limit_bytes=48 * 1024 * 1024
        ),
        name="adapter_step",
    )(*(
        pltpu.with_memory_space_constraint(arg, pltpu.HBM)
        for arg in (
            learn_acts, cotangent, base_weight, down_factor, up_factor.T, decode_acts
        )
    ))
    decoded, ga, nd, nu = pl.pallas_call(
        finish_kernel,
        out_shape=(
            sds((512, 1024), BF), sds((512, 512), BF), sds((2, 512), F32), sds((2, 64), F32),
        ),
        in_specs=[vmem] * 6,
        out_specs=(hbm,) * 4,
        scratch_shapes=[V((512, 1024), BF), pltpu.SemaphoreType.DMA((7,))],
        compiler_params=pltpu.CompilerParams(vmem_limit_bytes=16 * 1024 * 1024),
        name="finish",
    )(m, ld, nut, ga, nd, nu)
    return (ga, nd, nu, decoded)


def solution(mesh):
    in_specs = (
        P("dp", "tensor"),
        P("dp", None),
        P("tensor", None),
        P(None, "tensor"),
        P(),
        P("dp", "tensor"),
    )
    out_specs = (P("dp", "tensor"), P("dp", "tensor"), P(("dp", "tensor"), None), P("dp", None))
    return jax.shard_map(body, mesh=mesh, in_specs=in_specs, out_specs=out_specs, check_vma=False)
```
